256 devices in a mesh: dp: 16 (over y, x), expert: 16 (over z, core).
Axes of the slice: x: 4, y: 4, z: 8, core: 2. Of those that a mesh axis runs over, the one named last changes fastest.
Arguments:
- tokens: bfloat16 [32768, 2048], P(('dp', 'expert')), may hold values from -6 to 6
- grad_codes: bfloat16 [32768, 2048], P(('dp', 'expert')), may hold values from -6 to 6
- grad_scales: float32 [32768, 16], P(('dp', 'expert')), may hold values from 0.3 to 3
- modality: int32 [32768], P(('dp', 'expert')), may hold values from 0 to 1, as said below
- expert_ids: int32 [32768, 4], P(('dp', 'expert')), may hold values from 0 to 7, as said below
- combine: int32 [32768, 4], P(('dp', 'expert')), may hold values from 1 to 7
- w_gate: bfloat16 [16, 2048, 768], P('expert'), may hold values from -0.125 to 0.125
- w_up: bfloat16 [16, 2048, 768], P('expert'), may hold values from -0.125 to 0.125
- w_down: bfloat16 [16, 768, 2048], P('expert'), may hold values from -0.21875 to 0.21875
Outputs:
- input_grad: bfloat16 [32768, 2048], P(('dp', 'expert'))
- gate_grad: float32 [16, 2048, 768], P('expert', 'dp')
- up_grad: float32 [16, 2048, 768], P('expert', 'dp')
- down_grad: float32 [16, 768, 2048], P('expert', None, 'dp')
The draws below stay inside these ranges and needn't reach their ends.
Inputs may be any that keep to these rules, and one draw needn't show every extreme that they name: `modality`: independent of expert_ids' law only through the same draw: within one device's 128 tokens, between 7 and 9 sixteenths are text tokens, a multiple of 8 of each kind. `expert_ids`: A token's 4 ids are different. Within the rows of one device every expert of a modality is named equally often, so that no expert (id plus modality) is named by more than 36 rows of one device, and some expert is named by exactly 36 rows of some device.
All inputs are finite; a program needn't handle non-finite values.
Results may differ from the reference program's by a relative error of at most 0.025.
Values may be sent and summed in bfloat16 or wider, within the bound.
No kernel may reach another device: no remote copies, remote signals or barrier semaphores. Data moves between devices by JAX's collectives and lax.ppermute only.
A program may use at most 128 MiB of HBM per device.

```python
import math
import jax
import jax.numpy as jnp
from jax import lax

D = 2048
HW = 768
TOP = 4
TOK_DEV = 128
EXPERTS = 16
CAP = 36
TOKENS = 32768
N_DP = 16
N_EXPERT = 16


def routing(key):
    blocks = TOKENS // TOK_DEV
    per_mod = EXPERTS // 2
    unit = TOK_DEV // 16
    key_count, key_pick, key_order, key_text, key_image = jax.random.split(key, 5)
    counts = jax.random.randint(key_count, (blocks,), 7, 10)
    chosen = jax.random.randint(key_pick, (), 0, blocks)
    counts = jnp.where(jnp.arange(blocks) == chosen, 9, counts)
    text_rows = counts * unit
    orders = jax.vmap(lambda sub: jax.random.permutation(sub, TOK_DEV))(jax.random.split(key_order, blocks))
    position = jnp.argsort(orders, axis=1).astype(jnp.int32)
    labels_text = jax.vmap(lambda sub: jax.random.permutation(sub, per_mod))(jax.random.split(key_text, blocks))
    labels_image = jax.vmap(lambda sub: jax.random.permutation(sub, per_mod))(jax.random.split(key_image, blocks))
    is_image = (position >= text_rows[:, None]).astype(jnp.int32)
    local = position - is_image * text_rows[:, None]
    cyclic = (local[:, :, None] + jnp.arange(TOP, dtype=jnp.int32)[None, None, :]) % per_mod
    text_ids = jax.vmap(lambda labels, where_at: labels[where_at])(labels_text, cyclic)
    image_ids = jax.vmap(lambda labels, where_at: labels[where_at])(labels_image, cyclic)
    chosen_ids = jnp.where(is_image[:, :, None] == 1, image_ids, text_ids)
    return (is_image.reshape(TOKENS).astype(jnp.int32), chosen_ids.reshape(TOKENS, TOP).astype(jnp.int32))


def draw_modality(key, part):
    flags, chosen_ids = routing(key)
    return flags


def draw_expert_ids(key, part):
    flags, chosen_ids = routing(key)
    return chosen_ids


def place_ends(values, rng, low, high):
    spot = [jax.random.randint(jax.random.fold_in(rng, axis), (), 0, length) for axis, length in enumerate(values.shape)]
    longest = values.shape.index(max(values.shape))
    next_to = spot[:longest] + [(spot[longest] + 1) % values.shape[longest]] + spot[longest + 1:]
    return values.at[tuple(spot)].set(low).at[tuple(next_to)].set(high)


def steps_of(own_key, extent, cuts, smallest, high):
    factor_of = 1.0
    for axis_at, blocks in cuts:
        heights = jax.random.uniform(jax.random.fold_in(jax.random.fold_in(own_key, 6), axis_at), (blocks,), jnp.float32, smallest / len(cuts), high / len(cuts))
        factor_of = factor_of * jnp.repeat(jnp.exp(heights), extent[axis_at] // blocks).reshape((-1,) + (1,) * (len(extent) - 1 - axis_at))
    return factor_of


def normal_values(stream_key, extent, scale, most, pieces=(), kind=jnp.bfloat16):
    gain = steps_of(stream_key, extent, pieces, -0.22, 0.18) if pieces else 1.0
    values = jax.random.normal(stream_key, extent, jnp.float32) * scale * gain
    return jnp.minimum(jnp.maximum(values, -most), most).astype(kind)


def setup_inputs(seed: int = 0) -> dict:
    key_of = jax.random.split(jax.random.key(seed), 10)
    return {
        "tokens": normal_values(key_of[0], (TOKENS, D), 1.0, 6.0, ((0, 256),)),
        "grad_codes": normal_values(key_of[1], (TOKENS, D), 1.0, 6.0, ((0, 256),)),
        "grad_scales": jnp.clip(jnp.exp(math.log(3.0) - 2.3025851 * jax.random.uniform(key_of[2], (TOKENS, D // 128), jnp.float32) ** steps_of(key_of[2], (TOKENS, D // 128), ((0, 256),), -0.2, 0.2)), 0.3, 3.0),
        "modality": draw_modality(jax.random.fold_in(key_of[9], 71), 0),
        "expert_ids": draw_expert_ids(jax.random.fold_in(key_of[9], 71), 0),
        "combine": place_ends(jax.random.randint(key_of[5], (TOKENS, TOP), 1, 8), jax.random.fold_in(key_of[5], 1), 1, 7).astype(jnp.int32),
        "w_gate": normal_values(key_of[6], (EXPERTS, D, HW), D ** -0.5, 0.125, ((0, 16),)),
        "w_up": normal_values(key_of[7], (EXPERTS, D, HW), D ** -0.5, 0.125, ((0, 16),)),
        "w_down": normal_values(key_of[8], (EXPERTS, HW, D), HW ** -0.5, 0.21875, ((0, 16),)),
    }


def reference(tokens, grad_codes, grad_scales, modality, expert_ids, combine, w_gate, w_up, w_down):
    per_mod = EXPERTS // 2
    group = TOK_DEV * N_EXPERT
    buffer = N_EXPERT * CAP
    numer = combine.astype(jnp.float32)
    shares = numer / jnp.sum(numer, axis=1, keepdims=True)
    targets = expert_ids + per_mod * modality[:, None]

    def per_group(sums, index):
        start = (index * group).astype(jnp.int32)
        grp_tokens = lax.dynamic_slice_in_dim(tokens, start, group, 0)
        grp_codes = lax.dynamic_slice_in_dim(grp_codes_src := grad_codes, start, group, 0)
        grp_scales = lax.dynamic_slice_in_dim(grad_scales, start, group, 0)
        flat_target = lax.dynamic_slice_in_dim(targets, start, group, 0).reshape(-1)
        flat_share = lax.dynamic_slice_in_dim(shares, start, group, 0).reshape(-1)

        def per_expert(accum, expert):
            order = jnp.argsort((flat_target != expert).astype(jnp.int32), stable=True)[:buffer]
            valid = flat_target[order] == expert
            token_of = order // TOP
            inputs = jnp.where(valid[:, None], grp_tokens[token_of], jnp.zeros((), jnp.bfloat16))
            codes = grp_codes[token_of].astype(jnp.float32).reshape(buffer, D // 128, 128)
            dequant = (codes * grp_scales[token_of][:, :, None]).reshape(buffer, D)
            weight_of = jnp.where(valid, flat_share[order], jnp.zeros((), jnp.float32))
            grad_out = (weight_of[:, None] * dequant).astype(jnp.bfloat16)
            gate_w = w_gate[expert]
            up_w = w_up[expert]
            down_w = w_down[expert]
            gate = jnp.dot(inputs, gate_w, preferred_element_type=jnp.float32)
            upv = jnp.dot(inputs, up_w, preferred_element_type=jnp.float32)
            sigm = jax.nn.sigmoid(gate)
            act = (gate * sigm * upv).astype(jnp.bfloat16)
            grad_act = jnp.dot(grad_out, down_w.T, preferred_element_type=jnp.float32)
            grad_gate = (grad_act * upv * sigm * (1.0 + gate * (1.0 - sigm))).astype(jnp.bfloat16)
            grad_up = (grad_act * gate * sigm).astype(jnp.bfloat16)
            pair_grad = (jnp.dot(grad_gate, gate_w.T, preferred_element_type=jnp.float32)
                         + jnp.dot(grad_up, up_w.T, preferred_element_type=jnp.float32)).astype(jnp.bfloat16)
            added = jnp.where(valid[:, None], pair_grad.astype(jnp.float32), jnp.zeros((), jnp.float32))
            accum = accum.at[token_of].add(added)
            part_gate = jnp.dot(inputs.T, grad_gate, preferred_element_type=jnp.float32).astype(jnp.bfloat16)
            part_up = jnp.dot(inputs.T, grad_up, preferred_element_type=jnp.float32).astype(jnp.bfloat16)
            part_down = jnp.dot(act.T, grad_out, preferred_element_type=jnp.float32).astype(jnp.bfloat16)
            return accum, (part_gate, part_up, part_down)

        accum, parts = lax.scan(per_expert, jnp.zeros((group, D), jnp.float32), jnp.arange(EXPERTS, dtype=jnp.int32))
        sums = tuple(total + piece.astype(jnp.float32) for total, piece in zip(sums, parts))
        return sums, accum.astype(jnp.bfloat16)

    init = (jnp.zeros((EXPERTS, D, HW), jnp.float32), jnp.zeros((EXPERTS, D, HW), jnp.float32),
            jnp.zeros((EXPERTS, HW, D), jnp.float32))
    sums, grads = lax.scan(per_group, init, jnp.arange(N_DP, dtype=jnp.int32))
    input_grad = grads.reshape(TOKENS, D)
    return input_grad, sums[0] / N_DP, sums[1] / N_DP, sums[2] / N_DP
```

```python
import functools
import jax
import jax.numpy as jnp
from jax import lax
from jax.experimental import pallas as pl
from jax.experimental.pallas import tpu as pltpu
from jax.sharding import PartitionSpec as P

F32 = jnp.float32
BF16 = jnp.bfloat16
MB = 1024 * 1024

MAIN = 32
REST = 4
QUARTERS = 4
QCOLS = 512
SLAB = (MAIN + REST) * QUARTERS


def params(limit_mb):
    return pltpu.CompilerParams(vmem_limit_bytes=limit_mb * MB)


def iota(shape, dim):
    return lax.broadcasted_iota(jnp.int32, shape, dim)


def dot(a, b, dims=((1,), (0,))):
    return lax.dot_general(a, b, (dims, ((), ())), preferred_element_type=F32)


def quarter(q):
    return slice(q * QCOLS, (q + 1) * QCOLS)


def routing(meta_ref):
    n_tok = meta_ref.shape[1]
    mod = meta_ref[8:9, :]
    experts = iota((16, n_tok), 0)
    member = jnp.zeros((16, n_tok), F32)
    numer = jnp.zeros((16, n_tok), F32)
    denom = jnp.zeros((1, n_tok), F32)
    for k in range(4):
        hit = (meta_ref[k : k + 1, :] + 8 * mod) == experts
        weight = meta_ref[4 + k : 5 + k, :].astype(F32)
        member = member + jnp.where(hit, 1.0, 0.0)
        numer = numer + jnp.where(hit, weight, 0.0)
        denom = denom + weight
    earlier = jnp.where(iota((n_tok, n_tok), 0) < iota((n_tok, n_tok), 1), 1.0, 0.0)
    rank = dot(member.astype(BF16), earlier.astype(BF16))
    key = jnp.where(member > 0.5, rank, -1.0).astype(jnp.int32)
    return key, numer / denom


def pick_matrix(key):
    n_tok = key.shape[1]
    row = iota((MAIN + 16, n_tok), 0)
    want = jnp.where(row < MAIN, row, MAIN + row % REST)
    rows = [
        jnp.where(key[e : e + 1, :] == want, 1.0, 0.0) for e in range(key.shape[0])
    ]
    return jnp.concatenate(rows, axis=0)


def write_slabs(out_ref, picked):
    step = MAIN + 16
    which = iota((16, QCOLS), 0) // REST
    for e in range(16):
        base = e * step
        last = picked[base + MAIN : base + step]
        rest = last[:, quarter(0)]
        for q in range(QUARTERS):
            out_ref[e, q * MAIN : (q + 1) * MAIN, :] = picked[
                base : base + MAIN, quarter(q)
            ].astype(BF16)
            if q:
                rest = jnp.where(which == q, last[:, quarter(q)], rest)
        out_ref[e, QUARTERS * MAIN : SLAB, :] = rest.astype(BF16)


def dispatch_tokens_kernel(meta_ref, tokens_ref, out_ref):
    key, _ = routing(meta_ref)
    pick = pick_matrix(key).astype(BF16)
    write_slabs(out_ref, dot(pick, tokens_ref[...]))


def dispatch_grads_kernel(meta_ref, codes_ref, scales_ref, out_ref):
    key, share = routing(meta_ref)
    pick = pick_matrix(key)
    step = MAIN + 16
    weighted = jnp.concatenate(
        [pick[e * step : (e + 1) * step] * share[e : e + 1, :] for e in range(16)],
        axis=0,
    )
    factor = lax.dot_general(
        weighted,
        scales_ref[...],
        (((1,), (0,)), ((), ())),
        precision=lax.Precision.HIGHEST,
        preferred_element_type=F32,
    )
    picked = dot(pick.astype(BF16), codes_ref[...])
    scaled = [
        picked[:, b * 128 : (b + 1) * 128] * factor[:, b : b + 1]
        for b in range(factor.shape[1])
    ]
    write_slabs(out_ref, jnp.concatenate(scaled, axis=1))


def rest_select(q):
    row = iota((64, 256), 0)
    col = iota((64, 256), 1)
    return jnp.where(col == (row // REST) * 16 + REST * q + row % REST, 1.0, 0.0)


def unpack(slab_ref, rows_ref):
    rest = jnp.concatenate([slab_ref[s, QUARTERS * MAIN : SLAB, :] for s in range(16)], axis=0)
    for q in range(QUARTERS):
        for s in range(16):
            rows_ref[s * MAIN : (s + 1) * MAIN, quarter(q)] = slab_ref[
                s, q * MAIN : (q + 1) * MAIN, :
            ]
        rows_ref[16 * MAIN :, quarter(q)] = dot(rest_select(q).astype(BF16), rest).astype(BF16)


def forward_kernel(slab_ref, gate_ref, up_ref, rows_ref, act_ref, dgate_ref, dup_ref):
    @pl.when(pl.program_id(0) == 0)
    def _():
        unpack(slab_ref, rows_ref)

    rows = rows_ref[...]
    gate = dot(rows, gate_ref[...])
    upv = dot(rows, up_ref[...])
    sigm = jax.nn.sigmoid(gate)
    silu = gate * sigm
    act_ref[...] = (silu * upv).astype(BF16)
    dgate_ref[...] = upv * sigm * (1.0 + gate * (1.0 - sigm))
    dup_ref[...] = silu


def pair_kernel(
    rows_ref, down_ref, gate_ref, up_ref, dgate_ref, dup_ref, slab_ref, gg_ref, gu_ref, total
):
    step = pl.program_id(0)
    grad_act = dot(rows_ref[...], down_ref[...], ((1,), (1,)))
    gg = (grad_act * dgate_ref[...]).astype(BF16)
    gu = (grad_act * dup_ref[...]).astype(BF16)
    gg_ref[...] = gg
    gu_ref[...] = gu
    part = dot(gg, gate_ref[...], ((1,), (1,))) + dot(gu, up_ref[...], ((1,), (1,)))

    @pl.when(step == 0)
    def _():
        total[...] = part

    @pl.when(step > 0)
    def _():
        total[...] += part

    @pl.when(step == pl.num_programs(0) - 1)
    def _():
        rest = jnp.zeros((256, QCOLS), F32)
        for q in range(QUARTERS):
            for s in range(16):
                slab_ref[s, q * MAIN : (q + 1) * MAIN, :] = total[
                    s * MAIN : (s + 1) * MAIN, quarter(q)
                ].astype(BF16)
            rest += dot(
                rest_select(q).astype(BF16), total[16 * MAIN :, quarter(q)].astype(BF16), ((0,), (0,))
            )
        for s in range(16):
            slab_ref[s, QUARTERS * MAIN : SLAB, :] = rest[s * 16 : (s + 1) * 16].astype(BF16)


def combine_kernel(meta_ref, slab_ref, out_ref):
    key, _ = routing(meta_ref)
    n_tok = key.shape[1]
    row = iota((MAIN, n_tok), 0)
    main = jnp.concatenate(
        [jnp.where(key[e : e + 1, :] == row, 1.0, 0.0) for e in range(16)], axis=0
    ).astype(BF16)
    last = iota((16, n_tok), 0)
    rest_rows = jnp.concatenate(
        [slab_ref[e, QUARTERS * MAIN : SLAB, :] for e in range(16)], axis=0
    )
    for q in range(QUARTERS):
        rows = jnp.concatenate(
            [slab_ref[e, q * MAIN : (q + 1) * MAIN, :] for e in range(16)], axis=0
        )
        want = jnp.where(last // REST == q, MAIN + last % REST, -2)
        rest = jnp.concatenate(
            [jnp.where(key[e : e + 1, :] == want, 1.0, 0.0) for e in range(16)], axis=0
        ).astype(BF16)
        total = dot(main, rows, ((0,), (0,))) + dot(rest, rest_rows, ((0,), (0,)))
        out_ref[:, quarter(q)] = total.astype(BF16)


def plane_pieces(place_ref, big_ref, small_ref, first, outs):
    half = small_ref.shape[1] // 2
    part = half // 2
    here = (place_ref[0], place_ref[1])
    for way in range(2):
        up_ref, dn_ref, one_ref, three_ref, own_ref = outs[5 * way : 5 * way + 5]
        small_t = jnp.transpose(small_ref[:, way * half : (way + 1) * half].astype(F32)).astype(BF16)
        for near in range(4):
            for other in range(0, 4, 2):
                blocks = []
                for o in (other, other + 1):
                    ry, rx = (o, near) if way == 0 else (near, o)
                    block = lax.rem(here[0] + ry, 4) * 4 + lax.rem(here[1] + rx, 4)
                    blocks.append(big_ref[:, pl.ds(pl.multiple_of(block * 128, 128), 128)])
                piece = dot(small_t, jnp.concatenate(blocks, axis=1)).astype(BF16)
                for i in range(2):
                    value = piece[:, i * 128 : (i + 1) * 128]
                    o = other + i
                    if near == 2:
                        up_ref[o] = value[:part]
                        dn_ref[o] = value[part:]
                    else:
                        (own_ref, one_ref, None, three_ref)[near][o] = value


def piece_shapes(hidden):
    half = hidden // 2
    one = [(4, half // 2, 128)] * 2 + [(4, half, 128)] * 3
    return [jax.ShapeDtypeStruct(s, BF16) for s in one + one]


def down_kernel(place_ref, slab_ref, act_ref, rows_ref, *outs):
    unpack(slab_ref, rows_ref)
    plane_pieces(place_ref, rows_ref, act_ref, 0, outs)


def gate_up_kernel(place_ref, rows_ref, gg_ref, gu_ref, *refs):
    outs, small = refs[:10], refs[10]
    hidden = gg_ref.shape[1]
    small[:, :hidden] = gg_ref[...]
    small[:, hidden:] = gu_ref[...]
    plane_pieces(place_ref, rows_ref, small, 0, outs)


def plane_permute(value, along, shift):
    if along == "x":
        perm = [(i, (i // 4) * 4 + (i + shift) % 4) for i in range(16)]
    else:
        perm = [(i, (i + 4 * shift) % 16) for i in range(16)]
    return lax.ppermute(value, "dp", perm)


def add(*values):
    return sum(v.astype(F32) for v in values)


def ring_sum(pieces, along):
    up, dn, one, three, own = pieces
    part = up.shape[-2]
    from_low = plane_permute(up, along, 1)
    from_high = plane_permute(dn, along, -1)
    one = jnp.concatenate(
        [add(one[..., :part, :], from_low).astype(BF16), one[..., part:, :]], axis=-2
    )
    three = jnp.concatenate(
        [three[..., :part, :], add(three[..., part:, :], from_high).astype(BF16)], axis=-2
    )
    low = plane_permute(one, along, 1)
    high = plane_permute(three, along, -1)
    return add(own, low, high)


def plane_sum(pieces, along):
    other = "y" if along == "x" else "x"
    kept = ring_sum(pieces, along).astype(BF16)
    part = kept.shape[1] // 2
    return ring_sum(
        (kept[2, :part], kept[2, part:], kept[1], kept[3], kept[0]), other
    )


def exchange(value):
    return lax.all_to_all(value, "expert", split_axis=0, concat_axis=0, tiled=True)


def per_device(
    tokens, grad_codes, grad_scales, modality, expert_ids, combine, w_gate, w_up, w_down
):
    n_tok, width = tokens.shape
    hidden = w_gate.shape[2]
    rows = 16 * (MAIN + REST)
    n_data = lax.axis_size("dp")
    dp_at = lax.axis_index("dp")
    place = jnp.stack([dp_at // 4, dp_at % 4]).astype(jnp.int32)
    meta = jnp.concatenate([expert_ids.T, combine.T, modality[None, :]], axis=0)
    gate_w, up_w, down_w = w_gate[0], w_up[0], w_down[0]
    slabs = jax.ShapeDtypeStruct((16, SLAB, QCOLS), BF16)
    batch = jax.ShapeDtypeStruct((rows, width), BF16)

    send_tokens = pl.pallas_call(
        dispatch_tokens_kernel, out_shape=slabs, compiler_params=params(32), name="dispatch_tokens"
    )(meta, tokens)
    send_grads = pl.pallas_call(
        dispatch_grads_kernel, out_shape=slabs, compiler_params=params(32), name="dispatch_grads"
    )(meta, grad_codes, grad_scales)
    in_tokens = exchange(send_tokens)
    in_grads = exchange(send_grads)

    block = 256
    steps = hidden // block
    whole = lambda shape: pl.BlockSpec(shape, lambda i: (0,) * len(shape))
    by_col = lambda n: pl.BlockSpec((n, block), lambda i: (0, i))
    by_row = lambda n: pl.BlockSpec((block, n), lambda i: (i, 0))
    in_rows, act, dgate, dup = pl.pallas_call(
        forward_kernel,
        grid=(steps,),
        in_specs=[whole((16, SLAB, QCOLS)), by_col(width), by_col(width)],
        out_specs=[whole((rows, width)), by_col(rows), by_col(rows), by_col(rows)],
        out_shape=[
            batch,
            jax.ShapeDtypeStruct((rows, hidden), BF16),
            jax.ShapeDtypeStruct((rows, hidden), F32),
            jax.ShapeDtypeStruct((rows, hidden), F32),
        ],
        compiler_params=params(40),
        name="forward",
    )(in_tokens, gate_w, up_w)

    smem = pl.BlockSpec(memory_space=pltpu.SMEM)
    vmem = pl.BlockSpec(memory_space=pltpu.VMEM)
    grad_rows, *down_pieces = pl.pallas_call(
        down_kernel,
        in_specs=[smem, vmem, vmem],
        out_specs=[vmem] * 11,
        out_shape=[batch] + piece_shapes(hidden),
        compiler_params=params(40),
        name="down_partials",
    )(place, in_grads, act)

    pair_slabs, grad_gate, grad_up = pl.pallas_call(
        pair_kernel,
        grid=(steps,),
        in_specs=[
            whole((rows, width)),
            by_row(width),
            by_col(width),
            by_col(width),
            by_col(rows),
            by_col(rows),
        ],
        out_specs=[whole((16, SLAB, QCOLS)), by_col(rows), by_col(rows)],
        out_shape=[
            slabs,
            jax.ShapeDtypeStruct((rows, hidden), BF16),
            jax.ShapeDtypeStruct((rows, hidden), BF16),
        ],
        scratch_shapes=[pltpu.VMEM((rows, width), F32)],
        compiler_params=params(48),
        name="pair_grads",
    )(grad_rows, down_w, gate_w, up_w, dgate, dup)
    returned = exchange(pair_slabs)

    gate_up_pieces = pl.pallas_call(
        gate_up_kernel,
        in_specs=[smem, vmem, vmem, vmem],
        out_specs=[vmem] * 10,
        out_shape=piece_shapes(2 * hidden),
        scratch_shapes=[pltpu.VMEM((rows, 2 * hidden), BF16)],
        compiler_params=params(48),
        name="gate_up_partials",
    )(place, in_rows, grad_gate, grad_up)

    down_a = plane_sum(down_pieces[:5], "x")
    down_b = plane_sum(down_pieces[5:], "y")
    gate_t = plane_sum(gate_up_pieces[:5], "x")
    up_t = plane_sum(gate_up_pieces[5:], "y")

    input_grad = pl.pallas_call(
        combine_kernel,
        out_shape=jax.ShapeDtypeStruct((n_tok, width), BF16),
        compiler_params=params(32),
        name="combine",
    )(meta, returned)
    scale = 1.0 / n_data
    down_grad = jnp.concatenate([down_a, down_b], axis=0) * scale
    return (
        input_grad,
        (gate_t.T * scale)[None],
        (up_t.T * scale)[None],
        down_grad[None],
    )


def solution(mesh):
    in_specs = (
        P(("dp", "expert"), None),
        P(("dp", "expert"), None),
        P(("dp", "expert"), None),
        P(("dp", "expert")),
        P(("dp", "expert"), None),
        P(("dp", "expert"), None),
        P("expert", None, None),
        P("expert", None, None),
        P("expert", None, None),
    )
    out_specs = (
        P(("dp", "expert"), None),
        P("expert", "dp", None),
        P("expert", "dp", None),
        P("expert", None, "dp"),
    )
    return jax.shard_map(
        per_device, mesh=mesh, in_specs=in_specs, out_specs=out_specs, check_vma=False
    )
```

```python
import functools
import jax
import jax.numpy as jnp
from jax import lax
from jax.experimental import pallas as pl
from jax.experimental.pallas import tpu as pltpu
from jax.sharding import PartitionSpec as P

F32 = jnp.float32
BF16 = jnp.bfloat16
MB = 1024 * 1024

MAIN = 32
REST = 4
QUARTERS = 4
QCOLS = 512
SLAB = (MAIN + REST) * QUARTERS


def params(limit_mb):
    return pltpu.CompilerParams(vmem_limit_bytes=limit_mb * MB)


def iota(shape, dim):
    return lax.broadcasted_iota(jnp.int32, shape, dim)


def dot(a, b, dims=((1,), (0,))):
    return lax.dot_general(a, b, (dims, ((), ())), preferred_element_type=F32)


def quarter(q):
    return slice(q * QCOLS, (q + 1) * QCOLS)


def routing(meta_ref):
    n_tok = meta_ref.shape[1]
    mod = meta_ref[8:9, :]
    experts = iota((16, n_tok), 0)
    member = jnp.zeros((16, n_tok), F32)
    numer = jnp.zeros((16, n_tok), F32)
    denom = jnp.zeros((1, n_tok), F32)
    for k in range(4):
        hit = (meta_ref[k : k + 1, :] + 8 * mod) == experts
        weight = meta_ref[4 + k : 5 + k, :].astype(F32)
        member = member + jnp.where(hit, 1.0, 0.0)
        numer = numer + jnp.where(hit, weight, 0.0)
        denom = denom + weight
    earlier = jnp.where(iota((n_tok, n_tok), 0) < iota((n_tok, n_tok), 1), 1.0, 0.0)
    rank = dot(member.astype(BF16), earlier.astype(BF16))
    key = jnp.where(member > 0.5, rank, -1.0).astype(jnp.int32)
    return key, numer / denom


def pick_matrix(key):
    n_tok = key.shape[1]
    row = iota((MAIN + 16, n_tok), 0)
    want = jnp.where(row < MAIN, row, MAIN + row % REST)
    rows = [
        jnp.where(key[e : e + 1, :] == want, 1.0, 0.0) for e in range(key.shape[0])
    ]
    return jnp.concatenate(rows, axis=0)


def write_slabs(out_ref, picked):
    step = MAIN + 16
    which = iota((16, QCOLS), 0) // REST
    for e in range(16):
        base = e * step
        last = picked[base + MAIN : base + step]
        rest = last[:, quarter(0)]
        for q in range(QUARTERS):
            out_ref[e, q * MAIN : (q + 1) * MAIN, :] = picked[
                base : base + MAIN, quarter(q)
            ].astype(BF16)
            if q:
                rest = jnp.where(which == q, last[:, quarter(q)], rest)
        out_ref[e, QUARTERS * MAIN : SLAB, :] = rest.astype(BF16)


def dispatch_tokens_kernel(meta_ref, tokens_ref, out_ref):
    key, _ = routing(meta_ref)
    pick = pick_matrix(key).astype(BF16)
    write_slabs(out_ref, dot(pick, tokens_ref[...]))


def dispatch_grads_kernel(meta_ref, codes_ref, scales_ref, out_ref):
    key, share = routing(meta_ref)
    pick = pick_matrix(key)
    step = MAIN + 16
    weighted = jnp.concatenate(
        [pick[e * step : (e + 1) * step] * share[e : e + 1, :] for e in range(16)],
        axis=0,
    )
    factor = lax.dot_general(
        weighted,
        scales_ref[...],
        (((1,), (0,)), ((), ())),
        precision=lax.Precision.HIGHEST,
        preferred_element_type=F32,
    )
    picked = dot(pick.astype(BF16), codes_ref[...])
    scaled = [
        picked[:, b * 128 : (b + 1) * 128] * factor[:, b : b + 1]
        for b in range(factor.shape[1])
    ]
    write_slabs(out_ref, jnp.concatenate(scaled, axis=1))


def rest_select(q):
    row = iota((64, 256), 0)
    col = iota((64, 256), 1)
    return jnp.where(col == (row // REST) * 16 + REST * q + row % REST, 1.0, 0.0)


def unpack(slab_ref, rows_ref):
    rest = jnp.concatenate([slab_ref[s, QUARTERS * MAIN : SLAB, :] for s in range(16)], axis=0)
    for q in range(QUARTERS):
        for s in range(16):
            rows_ref[s * MAIN : (s + 1) * MAIN, quarter(q)] = slab_ref[
                s, q * MAIN : (q + 1) * MAIN, :
            ]
        rows_ref[16 * MAIN :, quarter(q)] = dot(rest_select(q).astype(BF16), rest).astype(BF16)


def forward_kernel(slab_ref, gate_ref, up_ref, rows_ref, act_ref, dgate_ref, dup_ref):
    @pl.when(pl.program_id(0) == 0)
    def _():
        unpack(slab_ref, rows_ref)

    rows = rows_ref[...]
    gate = dot(rows, gate_ref[...])
    upv = dot(rows, up_ref[...])
    sigm = jax.nn.sigmoid(gate)
    silu = gate * sigm
    act_ref[...] = (silu * upv).astype(BF16)
    dgate_ref[...] = upv * sigm * (1.0 + gate * (1.0 - sigm))
    dup_ref[...] = silu


def hidden_grad_kernel(
    place_ref, slab_ref, down_ref, dgate_ref, dup_ref, act_ref, in_rows_ref,
    rows_ref, gg_ref, gu_ref, *outs
):
    unpack(slab_ref, rows_ref)
    rows = rows_ref[...]
    block = 256
    for h in range(down_ref.shape[0] // block):
        cols = slice(h * block, (h + 1) * block)
        grad_act = dot(rows, down_ref[cols, :], ((1,), (1,)))
        gg_ref[:, cols] = (grad_act * dgate_ref[:, cols]).astype(BF16)
        gu_ref[:, cols] = (grad_act * dup_ref[:, cols]).astype(BF16)
    for way in range(2):
        plane_pieces(
            place_ref, in_rows_ref, rows_ref, act_ref, gg_ref, gu_ref, way, (2,),
            {2: outs[2 * way : 2 * way + 2]},
        )


def near_pieces_kernel(
    place_ref, in_rows_ref, rows_ref, act_ref, gg_ref, gu_ref, *outs
):
    for way in range(2):
        one, three, own = outs[3 * way : 3 * way + 3]
        plane_pieces(
            place_ref, in_rows_ref, rows_ref, act_ref, gg_ref, gu_ref, way, (1, 3, 0),
            {1: (one,), 3: (three,), 0: (own,)},
        )


def pair_kernel(gg_ref, gu_ref, gate_ref, up_ref, slab_ref, rest):
    q = pl.program_id(0)
    part = dot(gg_ref[...], gate_ref[...], ((1,), (1,))) + dot(
        gu_ref[...], up_ref[...], ((1,), (1,))
    )
    part = part.astype(BF16)
    base = pl.multiple_of(q * MAIN, MAIN)
    for s in range(16):
        slab_ref[s, pl.ds(base, MAIN), :] = part[s * MAIN : (s + 1) * MAIN]
    placed = dot(rest_select(q).astype(BF16), part[16 * MAIN :], ((0,), (0,)))

    @pl.when(q == 0)
    def _():
        rest[...] = placed

    @pl.when(q > 0)
    def _():
        rest[...] += placed

    @pl.when(q == QUARTERS - 1)
    def _():
        for s in range(16):
            slab_ref[s, QUARTERS * MAIN : SLAB, :] = rest[s * 16 : (s + 1) * 16].astype(BF16)


def combine_kernel(meta_ref, slab_ref, out_ref):
    key, _ = routing(meta_ref)
    n_tok = key.shape[1]
    row = iota((MAIN, n_tok), 0)
    main = jnp.concatenate(
        [jnp.where(key[e : e + 1, :] == row, 1.0, 0.0) for e in range(16)], axis=0
    ).astype(BF16)
    last = iota((16, n_tok), 0)
    rest_rows = jnp.concatenate(
        [slab_ref[e, QUARTERS * MAIN : SLAB, :] for e in range(16)], axis=0
    )
    for q in range(QUARTERS):
        rows = jnp.concatenate(
            [slab_ref[e, q * MAIN : (q + 1) * MAIN, :] for e in range(16)], axis=0
        )
        want = jnp.where(last // REST == q, MAIN + last % REST, -2)
        rest = jnp.concatenate(
            [jnp.where(key[e : e + 1, :] == want, 1.0, 0.0) for e in range(16)], axis=0
        ).astype(BF16)
        total = dot(main, rows, ((0,), (0,))) + dot(rest, rest_rows, ((0,), (0,)))
        out_ref[:, quarter(q)] = total.astype(BF16)


def plane_pieces(
    place_ref, in_rows_ref, grad_rows_ref, act_ref, gg_ref, gu_ref, way, nears, outs
):
    hidden = act_ref.shape[1]
    half = hidden // 2
    if way == 0:
        parts = ((act_ref[...], grad_rows_ref), (gg_ref[:, :half], in_rows_ref))
    else:
        parts = ((gg_ref[:, half:], in_rows_ref), (gu_ref[...], in_rows_ref))
    here = (place_ref[0], place_ref[1])
    at = 0
    for small, big_ref in parts:
        small_t = jnp.transpose(small)
        count = small_t.shape[0]
        for near in nears:
            blocks = []
            for o in range(4):
                ry, rx = (o, near) if way == 0 else (near, o)
                block = lax.rem(here[0] + ry, 4) * 4 + lax.rem(here[1] + rx, 4)
                blocks.append(big_ref[:, pl.ds(pl.multiple_of(block * 128, 128), 128)])
            piece = dot(small_t, jnp.concatenate(blocks, axis=1)).astype(BF16)
            for o in range(4):
                done = 0
                for ref in outs[near]:
                    start = max(at - done, 0)
                    stop = min(at + count - done, ref.shape[1])
                    if start < stop:
                        ref[o, start:stop, :] = piece[
                            start + done - at : stop + done - at, o * 128 : (o + 1) * 128
                        ]
                    done += ref.shape[1]
        at += count


def plane_permute(value, along, shift):
    if along == "x":
        perm = [(i, (i // 4) * 4 + (i + shift) % 4) for i in range(16)]
    else:
        perm = [(i, (i + 4 * shift) % 16) for i in range(16)]
    return lax.ppermute(value, "dp", perm)


def add_first_kernel(one_ref, got_ref, out_ref):
    part = got_ref.shape[1]
    out_ref[:, :part, :] = (one_ref[:, :part, :].astype(F32) + got_ref[...].astype(F32)).astype(BF16)
    out_ref[:, part:, :] = one_ref[:, part:, :]


def add_last_kernel(one_ref, got_ref, out_ref):
    part = got_ref.shape[1]
    out_ref[:, :part, :] = one_ref[:, :part, :]
    out_ref[:, part:, :] = (one_ref[:, part:, :].astype(F32) + got_ref[...].astype(F32)).astype(BF16)


def add_pieces(kernel, piece, got):
    return pl.pallas_call(
        kernel,
        out_shape=jax.ShapeDtypeStruct(piece.shape, BF16),
        input_output_aliases={0: 0},
        compiler_params=params(16),
        name="add_pieces",
    )(piece, got)


def sum_kernel(own_ref, low_ref, high_ref, k0_ref, k1_ref, k2_ref, k3_ref):
    for i, ref in enumerate((k0_ref, k1_ref, k2_ref, k3_ref)):
        total = own_ref[i].astype(F32) + low_ref[i].astype(F32) + high_ref[i].astype(F32)
        ref[...] = total.astype(ref.dtype)


def plane_sum(far, near, along):
    up, dn = far
    one, three, own = near
    other = "y" if along == "x" else "x"
    one = add_pieces(add_first_kernel, one, plane_permute(up, along, 1))
    three = add_pieces(add_last_kernel, three, plane_permute(dn, along, -1))
    low = plane_permute(one, along, 1)
    high = plane_permute(three, along, -1)
    shape = own.shape[1:]
    kept = pl.pallas_call(
        sum_kernel,
        out_shape=[jax.ShapeDtypeStruct(shape, F32)] + [jax.ShapeDtypeStruct(shape, BF16)] * 3,
        compiler_params=params(24),
        name="sum_pieces",
    )(own, low, high)
    return (
        kept[0],
        plane_permute(kept[1], other, 1),
        plane_permute(kept[2], other, 2),
        plane_permute(kept[3], other, -1),
    )


def finish_kernel(*refs):
    a_refs, b_refs, (gate_ref, up_ref, down_ref) = refs[:4], refs[4:8], refs[8:]
    hidden = down_ref.shape[0]
    half = hidden // 2
    scale = 1.0 / 16

    def total(parts, rows):
        return sum(p[rows, :].astype(F32) for p in parts) * scale

    down_ref[...] = total(a_refs, slice(0, hidden))
    gate_ref[:, :half] = jnp.transpose(total(a_refs, slice(hidden, hidden + half)))
    gate_ref[:, half:] = jnp.transpose(total(b_refs, slice(0, half)))
    up_ref[...] = jnp.transpose(total(b_refs, slice(half, half + hidden)))


def exchange(value):
    return lax.all_to_all(value, "expert", split_axis=0, concat_axis=0, tiled=True)


def per_device(
    tokens, grad_codes, grad_scales, modality, expert_ids, combine, w_gate, w_up, w_down
):
    n_tok, width = tokens.shape
    hidden = w_gate.shape[2]
    rows = 16 * (MAIN + REST)
    dp_at = lax.axis_index("dp")
    place = jnp.stack([dp_at // 4, dp_at % 4]).astype(jnp.int32)
    meta = jnp.concatenate([expert_ids.T, combine.T, modality[None, :]], axis=0)
    gate_w, up_w, down_w = w_gate[0], w_up[0], w_down[0]
    slabs = jax.ShapeDtypeStruct((16, SLAB, QCOLS), BF16)
    batch = jax.ShapeDtypeStruct((rows, width), BF16)

    send_tokens = pl.pallas_call(
        dispatch_tokens_kernel, out_shape=slabs, compiler_params=params(32), name="dispatch_tokens"
    )(meta, tokens)
    send_grads = pl.pallas_call(
        dispatch_grads_kernel, out_shape=slabs, compiler_params=params(32), name="dispatch_grads"
    )(meta, grad_codes, grad_scales)
    in_tokens = exchange(send_tokens)
    in_grads = exchange(send_grads)

    block = 256
    steps = hidden // block
    whole = lambda shape: pl.BlockSpec(shape, lambda i: (0,) * len(shape))
    by_col = lambda n: pl.BlockSpec((n, block), lambda i: (0, i))
    by_row = lambda n: pl.BlockSpec((block, n), lambda i: (i, 0))
    in_rows, act, dgate, dup = pl.pallas_call(
        forward_kernel,
        grid=(steps,),
        in_specs=[whole((16, SLAB, QCOLS)), by_col(width), by_col(width)],
        out_specs=[whole((rows, width)), by_col(rows), by_col(rows), by_col(rows)],
        out_shape=[
            batch,
            jax.ShapeDtypeStruct((rows, hidden), BF16),
            jax.ShapeDtypeStruct((rows, hidden), F32),
            jax.ShapeDtypeStruct((rows, hidden), F32),
        ],
        compiler_params=params(40),
        name="forward",
    )(in_tokens, gate_w, up_w)

    smem = pl.BlockSpec(memory_space=pltpu.SMEM)
    vmem = pl.BlockSpec(memory_space=pltpu.VMEM)
    bf = lambda *shape: jax.ShapeDtypeStruct(shape, BF16)
    each = 3 * hidden // 2
    grad_rows, grad_gate, grad_up, *far = pl.pallas_call(
        hidden_grad_kernel,
        in_specs=[smem] + [vmem] * 6,
        out_specs=[vmem] * 7,
        out_shape=[batch, bf(rows, hidden), bf(rows, hidden)] + [bf(4, each // 2, 128)] * 4,
        compiler_params=params(48),
        name="hidden_grads",
    )(place, in_grads, down_w, dgate, dup, act, in_rows)

    pair_slabs = pl.pallas_call(
        pair_kernel,
        grid=(QUARTERS,),
        in_specs=[
            whole((rows, hidden)),
            whole((rows, hidden)),
            pl.BlockSpec((QCOLS, hidden), lambda i: (i, 0)),
            pl.BlockSpec((QCOLS, hidden), lambda i: (i, 0)),
        ],
        out_specs=whole((16, SLAB, QCOLS)),
        out_shape=slabs,
        scratch_shapes=[pltpu.VMEM((256, QCOLS), F32)],
        compiler_params=params(32),
        name="pair_grads",
    )(grad_gate, grad_up, gate_w, up_w)
    returned = exchange(pair_slabs)

    near = pl.pallas_call(
        near_pieces_kernel,
        in_specs=[smem] + [vmem] * 5,
        out_specs=[vmem] * 6,
        out_shape=[bf(4, each, 128)] * 6,
        compiler_params=params(48),
        name="near_pieces",
    )(place, in_rows, grad_rows, act, grad_gate, grad_up)

    parts_a = plane_sum(far[:2], near[:3], "x")
    parts_b = plane_sum(far[2:], near[3:], "y")
    gate_grad, up_grad, down_grad = pl.pallas_call(
        finish_kernel,
        out_shape=[
            jax.ShapeDtypeStruct((128, hidden), F32),
            jax.ShapeDtypeStruct((128, hidden), F32),
            jax.ShapeDtypeStruct((hidden, 128), F32),
        ],
        compiler_params=params(24),
        name="finish",
    )(*parts_a, *parts_b)

    input_grad = pl.pallas_call(
        combine_kernel,
        out_shape=jax.ShapeDtypeStruct((n_tok, width), BF16),
        compiler_params=params(32),
        name="combine",
    )(meta, returned)
    return input_grad, gate_grad[None], up_grad[None], down_grad[None]


def solution(mesh):
    in_specs = (
        P(("dp", "expert"), None),
        P(("dp", "expert"), None),
        P(("dp", "expert"), None),
        P(("dp", "expert")),
        P(("dp", "expert"), None),
        P(("dp", "expert"), None),
        P("expert", None, None),
        P("expert", None, None),
        P("expert", None, None),
    )
    out_specs = (
        P(("dp", "expert"), None),
        P("expert", "dp", None),
        P("expert", "dp", None),
        P("expert", None, "dp"),
    )
    return jax.shard_map(
        per_device, mesh=mesh, in_specs=in_specs, out_specs=out_specs, check_vma=False
    )
```

```python
import functools
import jax
import jax.numpy as jnp
from jax import lax
from jax.experimental import pallas as pl
from jax.experimental.pallas import tpu as pltpu
from jax.sharding import PartitionSpec as P

F32 = jnp.float32
BF16 = jnp.bfloat16
MB = 1024 * 1024

MAIN = 32
REST = 4
QUARTERS = 4
QCOLS = 512
SLAB = (MAIN + REST) * QUARTERS


def params(limit_mb):
    return pltpu.CompilerParams(vmem_limit_bytes=limit_mb * MB)


def iota(shape, dim):
    return lax.broadcasted_iota(jnp.int32, shape, dim)


def dot(a, b, dims=((1,), (0,))):
    return lax.dot_general(a, b, (dims, ((), ())), preferred_element_type=F32)


def quarter(q):
    return slice(q * QCOLS, (q + 1) * QCOLS)


def routing(meta_ref):
    n_tok = meta_ref.shape[1]
    mod = meta_ref[8:9, :]
    experts = iota((16, n_tok), 0)
    member = jnp.zeros((16, n_tok), F32)
    numer = jnp.zeros((16, n_tok), F32)
    denom = jnp.zeros((1, n_tok), F32)
    for k in range(4):
        hit = (meta_ref[k : k + 1, :] + 8 * mod) == experts
        weight = meta_ref[4 + k : 5 + k, :].astype(F32)
        member = member + jnp.where(hit, 1.0, 0.0)
        numer = numer + jnp.where(hit, weight, 0.0)
        denom = denom + weight
    earlier = jnp.where(iota((n_tok, n_tok), 0) < iota((n_tok, n_tok), 1), 1.0, 0.0)
    rank = dot(member.astype(BF16), earlier.astype(BF16))
    key = jnp.where(member > 0.5, rank, -1.0).astype(jnp.int32)
    return key, numer / denom


EARLY = (0, 1, -1, 2, -2)
LATE = (3, -3, 4)
N_EARLY = MAIN * len(EARLY)
N_LATE = MAIN * len(LATE)
N_REST = REST * 8


def source_of(place_ref, back, same_core):
    z, core = place_ref[2], place_ref[3]
    return lax.rem(z - back + 8, 8) * 2 + (core if same_core else 1 - core)


def stamp_kernel(meta_ref, tokens_ref, out_ref):
    n_tok = tokens_ref.shape[0]
    out_ref[:n_tok, :] = tokens_ref[...]
    first = iota((8, n_tok), 0) == 0
    stamps = []
    for k in range(8):
        value = meta_ref[k : k + 1, :]
        if k < 4:
            value = value + 8 * meta_ref[8:9, :]
        stamps.append(jnp.where(first, value, 0).astype(F32))
    stamps.append(jnp.zeros((8, tokens_ref.shape[1] - 8 * n_tok), F32))
    out_ref[n_tok:, :] = jnp.concatenate(stamps, axis=1).astype(BF16)


def dequant_kernel(codes_ref, scales_ref, out_ref):
    for b in range(scales_ref.shape[1]):
        cols = slice(b * 128, (b + 1) * 128)
        out_ref[:, cols] = (codes_ref[:, cols].astype(F32) * scales_ref[:, b : b + 1]).astype(BF16)


def picks(place_ref, block_ref):
    n_tok = block_ref.shape[0] - 8
    stamp = block_ref[n_tok:, :].astype(F32)[0:1, :]
    z, core = place_ref[2], place_ref[3]
    row = iota((8, n_tok), 0)
    expert = (2 * z + jnp.where(row == 0, core, 1 - core)).astype(F32)
    member = jnp.zeros((8, n_tok), F32)
    numer = jnp.zeros((8, n_tok), F32)
    denom = jnp.zeros((1, n_tok), F32)
    for k in range(4):
        hit = stamp[:, k * n_tok : (k + 1) * n_tok] == expert
        weight = stamp[:, (4 + k) * n_tok : (5 + k) * n_tok]
        member = member + jnp.where(hit, 1.0, 0.0)
        numer = numer + jnp.where(hit, weight, 0.0)
        denom = denom + weight
    earlier = jnp.where(iota((n_tok, n_tok), 0) < iota((n_tok, n_tok), 1), 1.0, 0.0)
    rank = dot(member.astype(BF16), earlier.astype(BF16))
    return jnp.where(member > 0.5, rank, -1.0), numer / denom


def pick_rows(key, share, block, want):
    pick = jnp.concatenate(
        [jnp.where(key[i : i + 1, :] == want.astype(F32), 1.0, 0.0) for i in range(2)], axis=0
    )
    rows = dot(pick.astype(BF16), block)
    if share is not None:
        r = want.shape[0]
        factor = jnp.concatenate(
            [
                jnp.sum(pick[i * r : (i + 1) * r] * share[i : i + 1, :], axis=1, keepdims=True)
                for i in range(2)
            ],
            axis=0,
        )
        rows = rows * factor
    return rows


def rest_want(at, n_tok):
    row = iota((N_REST, n_tok), 0)
    return jnp.where(row // REST == at, MAIN + row % REST, -2)


def pick_blocks(first_at, info, blocks, own_ref, other_ref, rest):
    for i, ((key, share), block) in enumerate(zip(info, blocks)):
        n_tok = key.shape[1]
        want = jnp.concatenate(
            [iota((MAIN, n_tok), 0), rest_want(first_at + i, n_tok)], axis=0
        )
        rows = pick_rows(key, share, block, want)
        step = MAIN + N_REST
        own_ref[i * MAIN : (i + 1) * MAIN, :] = rows[:MAIN].astype(BF16)
        other_ref[i * MAIN : (i + 1) * MAIN, :] = rows[step : step + MAIN].astype(BF16)
        last = jnp.concatenate([rows[MAIN:step], rows[step + MAIN :]], axis=0)
        rest = last if rest is None else rest + last
    return rest


def pick_tokens_kernel(early, place_ref, *refs):
    backs = EARLY if early else LATE
    blocks = refs[: len(backs)]
    n_tok = blocks[0].shape[0] - 8
    info_ref = refs[-1]
    info = []
    for i, block in enumerate(blocks):
        key, share = picks(place_ref, block)
        info_ref[16 * i : 16 * i + 8, :] = key
        info_ref[16 * i + 8 : 16 * i + 16, :] = share
        info.append((key, None))
    pick_finish(early, info, [b[:n_tok, :] for b in blocks], refs[len(backs) : -1])


def pick_grads_kernel(early, *refs):
    backs = EARLY if early else LATE
    info_ref, blocks = refs[0], refs[1 : 1 + len(backs)]
    info = [
        (info_ref[16 * i : 16 * i + 8, :], info_ref[16 * i + 8 : 16 * i + 16, :])
        for i in range(len(backs))
    ]
    pick_finish(early, info, [b[...] for b in blocks], refs[1 + len(backs) :])


def pick_finish(early, info, blocks, refs):
    if early:
        own_ref, other_ref, rest_ref = refs
        rest_ref[...] = pick_blocks(0, info, blocks, own_ref, other_ref, None).astype(BF16)
    else:
        rest_ref, own_ref, other_ref = refs
        rest = pick_blocks(
            len(EARLY), info, blocks, own_ref, other_ref, rest_ref[...].astype(F32)
        )
        own_ref[N_LATE:, :] = rest[:N_REST].astype(BF16)
        other_ref[N_LATE:, :] = rest[N_REST:].astype(BF16)


def forward_kernel(own_ref, other_ref, gate_ref, up_ref, rows_ref, act_ref, dgate_ref, dup_ref):
    @pl.when(pl.program_id(0) == 0)
    def _():
        half = own_ref.shape[0]
        rows_ref[:half, :] = own_ref[...]
        rows_ref[half:, :] = other_ref[...]

    rows = rows_ref[...]
    gate = dot(rows, gate_ref[...])
    upv = dot(rows, up_ref[...])
    sigm = jax.nn.sigmoid(gate)
    silu = gate * sigm
    act_ref[...] = (silu * upv).astype(BF16)
    dgate_ref[...] = upv * sigm * (1.0 + gate * (1.0 - sigm))
    dup_ref[...] = silu


def hidden_grads(own_ref, other_ref, down_ref, dgate_ref, dup_ref, rows_ref, gg_ref, gu_ref):
    half = own_ref.shape[0]
    rows_ref[:half, :] = own_ref[...]
    rows_ref[half:, :] = other_ref[...]
    rows = rows_ref[...]
    block = 256
    for h in range(down_ref.shape[0] // block):
        cols = slice(h * block, (h + 1) * block)
        grad_act = dot(rows, down_ref[cols, :], ((1,), (1,)))
        gg_ref[:, cols] = (grad_act * dgate_ref[:, cols]).astype(BF16)
        gu_ref[:, cols] = (grad_act * dup_ref[:, cols]).astype(BF16)


def early_pieces_kernel(place_ref, *refs):
    batch, outs = refs[:5], refs[5:]
    for way in range(2):
        far, (one, three, own) = outs[2 * way : 2 * way + 2], outs[4 + 3 * way : 7 + 3 * way]
        plane_pieces(
            place_ref, batch, way, {2: far, 1: (one,), 3: (three,), 0: (own,)}, None
        )


def load_all(sources, targets, sems):
    copies = [
        pltpu.make_async_copy(source, target, sems.at[i])
        for i, (source, target) in enumerate(zip(sources, targets))
    ]
    for copy in copies:
        copy.start()
    return copies


def late_kernel(place_ref, *refs):
    tokens, grads, weights, far = refs[:2], refs[2:4], refs[4:7], refs[7:11]
    in_ref, grad_ref, act_ref, gg_ref, gu_ref = batch = refs[11:16]
    outs = refs[16:20]
    gate_v, up_v, down_v = refs[20:23]
    prior, weight_sems, far_sems = refs[23:27], refs[27], refs[28]
    hidden = down_v.shape[0]
    block = 256
    loads = []
    for h in range(hidden // block):
        cols = slice(h * block, (h + 1) * block)
        loads.append(
            [
                pltpu.make_async_copy(source.at[at], target.at[at], weight_sems.at[h, i])
                for i, (source, target, at) in enumerate(
                    (
                        (weights[0], gate_v, (slice(None), cols)),
                        (weights[1], up_v, (slice(None), cols)),
                        (weights[2], down_v, (cols, slice(None))),
                    )
                )
            ]
        )
        for copy in loads[h]:
            copy.start()
    far_loads = load_all(far, prior, far_sems)
    half = tokens[0].shape[0]
    for pair, ref in ((tokens, in_ref), (grads, grad_ref)):
        ref[:half, :] = pair[0][...]
        ref[half:, :] = pair[1][...]
    for h in range(hidden // block):
        cols = slice(h * block, (h + 1) * block)
        for copy in loads[h]:
            copy.wait()
        gate = dot(in_ref[...], gate_v[:, cols])
        upv = dot(in_ref[...], up_v[:, cols])
        grad_act = dot(grad_ref[...], down_v[cols, :], ((1,), (1,)))
        sigm = jax.nn.sigmoid(gate)
        silu = gate * sigm
        act_ref[:, cols] = (silu * upv).astype(BF16)
        gg_ref[:, cols] = (grad_act * upv * sigm * (1.0 + gate * (1.0 - sigm))).astype(BF16)
        gu_ref[:, cols] = (grad_act * silu).astype(BF16)
    for copy in far_loads:
        copy.wait()
    for way in range(2):
        part = slice(2 * way, 2 * way + 2)
        plane_pieces(place_ref, batch, way, {2: outs[part]}, {2: prior[part]})


def late_pieces_kernel(nears, place_ref, *refs):
    count = len(nears)
    batch, refs = refs[:5], refs[5:]
    sources, outs, prior, sems = (
        refs[: 2 * count],
        refs[2 * count : 4 * count],
        refs[4 * count : 6 * count],
        refs[6 * count],
    )
    copies = load_all(sources, prior, sems)
    for way in range(2):
        for copy in copies[count * way : count * way + count]:
            copy.wait()
        plane_pieces(
            place_ref,
            batch,
            way,
            {near: (outs[count * way + i],) for i, near in enumerate(nears)},
            {near: (prior[count * way + i],) for i, near in enumerate(nears)},
        )


def early_pair_kernel(gg_ref, gu_ref, gate_ref, up_ref, out_ref):
    part = dot(gg_ref[...], gate_ref[...], ((1,), (1,))) + dot(
        gu_ref[...], up_ref[...], ((1,), (1,))
    )
    out_ref[...] = part.astype(BF16)


def late_pair_kernel(place_ref, gg_ref, gu_ref, gate_ref, up_ref, early_ref, slab_ref, rest):
    q = pl.program_id(0)
    part = dot(gg_ref[...], gate_ref[...], ((1,), (1,))) + dot(
        gu_ref[...], up_ref[...], ((1,), (1,))
    )
    part = part.astype(BF16)
    base = pl.multiple_of(q * MAIN, MAIN)
    row = iota((128, N_REST), 0)
    col = iota((128, N_REST), 1)
    spread = jnp.where(
        (row // 16 == col // REST) & (row % 16 == REST * q + col % REST), 1.0, 0.0
    ).astype(BF16)
    for core in range(2):
        for at, back in enumerate(EARLY):
            to = source_of(place_ref, back, core == 0)
            start = core * N_EARLY + at * MAIN
            slab_ref[to, pl.ds(base, MAIN), :] = early_ref[start : start + MAIN, :]
        first = core * (N_LATE + N_REST)
        for at, back in enumerate(LATE):
            to = source_of(place_ref, back, core == 0)
            start = first + at * MAIN
            slab_ref[to, pl.ds(base, MAIN), :] = part[start : start + MAIN]
        placed = dot(spread, part[first + N_LATE : first + N_LATE + N_REST])
        rows = slice(core * 128, (core + 1) * 128)

        @pl.when(q == 0)
        def _():
            rest[rows, :] = placed

        @pl.when(q > 0)
        def _():
            rest[rows, :] += placed

        @pl.when(q == QUARTERS - 1)
        def _():
            for at, back in enumerate(EARLY + LATE):
                to = source_of(place_ref, back, core == 0)
                start = core * 128 + at * 16
                slab_ref[to, QUARTERS * MAIN : SLAB, :] = rest[start : start + 16, :].astype(BF16)


def combine_kernel(meta_ref, slab_ref, out_ref):
    key, _ = routing(meta_ref)
    n_tok = key.shape[1]
    row = iota((MAIN, n_tok), 0)
    main = jnp.concatenate(
        [jnp.where(key[e : e + 1, :] == row, 1.0, 0.0) for e in range(16)], axis=0
    ).astype(BF16)
    last = iota((16, n_tok), 0)
    rest_rows = jnp.concatenate(
        [slab_ref[e, QUARTERS * MAIN : SLAB, :] for e in range(16)], axis=0
    )
    for q in range(QUARTERS):
        rows = jnp.concatenate(
            [slab_ref[e, q * MAIN : (q + 1) * MAIN, :] for e in range(16)], axis=0
        )
        want = jnp.where(last // REST == q, MAIN + last % REST, -2)
        rest = jnp.concatenate(
            [jnp.where(key[e : e + 1, :] == want, 1.0, 0.0) for e in range(16)], axis=0
        ).astype(BF16)
        total = dot(main, rows, ((0,), (0,))) + dot(rest, rest_rows, ((0,), (0,)))
        out_ref[:, quarter(q)] = total.astype(BF16)


def plane_pieces(place_ref, batch, way, outs, prior):
    hidden = batch[2].shape[1]
    half = hidden // 2
    full = slice(0, hidden)
    if way == 0:
        parts = ((2, full, 1), (3, slice(0, half), 0))
    else:
        parts = ((3, slice(half, hidden), 0), (4, full, 0))
    here = (place_ref[0], place_ref[1])
    at = 0
    for small, cols, big in parts:
        small_t = jnp.transpose(batch[small][:, cols])
        count = cols.stop - cols.start
        for near in outs:
            blocks = []
            for o in range(4):
                ry, rx = (o, near) if way == 0 else (near, o)
                block = lax.rem(here[0] + ry, 4) * 4 + lax.rem(here[1] + rx, 4)
                blocks.append(batch[big][:, pl.ds(pl.multiple_of(block * 128, 128), 128)])
            piece = dot(small_t, jnp.concatenate(blocks, axis=1))
            for o in range(4):
                done = 0
                for i, ref in enumerate(outs[near]):
                    start = max(at - done, 0)
                    stop = min(at + count - done, ref.shape[1])
                    if start < stop:
                        value = piece[start + done - at : stop + done - at, o * 128 : (o + 1) * 128]
                        if prior is not None:
                            value = value + prior[near][i][o, start:stop, :].astype(F32)
                        ref[o, start:stop, :] = value.astype(BF16)
                    done += ref.shape[1]
        at += count


def plane_permute(value, along, shift):
    if along == "x":
        perm = [(i, (i // 4) * 4 + (i + shift) % 4) for i in range(16)]
    else:
        perm = [(i, (i + 4 * shift) % 16) for i in range(16)]
    return lax.ppermute(value, "dp", perm)


def add_first_kernel(one_ref, got_ref, out_ref):
    part = got_ref.shape[1]
    out_ref[:, :part, :] = (one_ref[:, :part, :].astype(F32) + got_ref[...].astype(F32)).astype(BF16)
    out_ref[:, part:, :] = one_ref[:, part:, :]


def add_last_kernel(one_ref, got_ref, out_ref):
    part = got_ref.shape[1]
    out_ref[:, :part, :] = one_ref[:, :part, :]
    out_ref[:, part:, :] = (one_ref[:, part:, :].astype(F32) + got_ref[...].astype(F32)).astype(BF16)


def add_pieces(kernel, piece, got):
    return pl.pallas_call(
        kernel,
        out_shape=jax.ShapeDtypeStruct(piece.shape, BF16),
        input_output_aliases={0: 0},
        compiler_params=params(16),
        name="add_pieces",
    )(piece, got)


def sum_kernel(own_ref, low_ref, high_ref, k0_ref, k1_ref, k2_ref, k3_ref):
    for i, ref in enumerate((k0_ref, k1_ref, k2_ref, k3_ref)):
        total = own_ref[i].astype(F32) + low_ref[i].astype(F32) + high_ref[i].astype(F32)
        ref[...] = total.astype(ref.dtype)


def plane_sum(one, three, own, along):
    other = "y" if along == "x" else "x"
    low = plane_permute(one, along, 1)
    high = plane_permute(three, along, -1)
    shape = own.shape[1:]
    kept = pl.pallas_call(
        sum_kernel,
        out_shape=[jax.ShapeDtypeStruct(shape, F32)] + [jax.ShapeDtypeStruct(shape, BF16)] * 3,
        compiler_params=params(24),
        name="sum_pieces",
    )(own, low, high)
    return (
        kept[0],
        plane_permute(kept[1], other, 1),
        plane_permute(kept[2], other, 2),
        plane_permute(kept[3], other, -1),
    )


def finish_kernel(*refs):
    a_refs, b_refs, (gate_ref, up_ref, down_ref) = refs[:4], refs[4:8], refs[8:]
    hidden = down_ref.shape[0]
    half = hidden // 2
    scale = 1.0 / 16

    def total(parts, rows):
        return sum(p[rows, :].astype(F32) for p in parts) * scale

    down_ref[...] = total(a_refs, slice(0, hidden))
    gate_ref[:, :half] = jnp.transpose(total(a_refs, slice(hidden, hidden + half)))
    gate_ref[:, half:] = jnp.transpose(total(b_refs, slice(0, half)))
    up_ref[...] = jnp.transpose(total(b_refs, slice(half, half + hidden)))


def exchange(value):
    return lax.all_to_all(value, "expert", split_axis=0, concat_axis=0, tiled=True)


def tie(held, backs, *others):
    tied = lax.optimization_barrier(tuple(held[b] for b in backs) + others)
    for b, value in zip(backs, tied):
        held[b] = value
    return tied[len(backs) :]


def ring_permute(value, shift):
    perm = [(i, ((i // 2 + shift) % 8) * 2 + i % 2) for i in range(16)]
    return lax.ppermute(value, "expert", perm)


def swap_cores(value):
    return lax.ppermute(value, "expert", [(i, i ^ 1) for i in range(16)])


def per_device(
    tokens, grad_codes, grad_scales, modality, expert_ids, combine, w_gate, w_up, w_down
):
    n_tok, width = tokens.shape
    hidden = w_gate.shape[2]
    dp_at = lax.axis_index("dp")
    ex_at = lax.axis_index("expert")
    place = jnp.stack([dp_at // 4, dp_at % 4, ex_at // 2, ex_at % 2]).astype(jnp.int32)
    meta = jnp.concatenate(
        [expert_ids.T, combine.T, modality[None, :], jnp.zeros((7, n_tok), jnp.int32)], axis=0
    )
    gate_w, up_w, down_w = w_gate[0], w_up[0], w_down[0]
    bf = lambda *shape: jax.ShapeDtypeStruct(shape, BF16)
    f32 = lambda *shape: jax.ShapeDtypeStruct(shape, F32)
    smem = pl.BlockSpec(memory_space=pltpu.SMEM)
    vmem = pl.BlockSpec(memory_space=pltpu.VMEM)
    block = 256
    steps = hidden // block
    whole = lambda *shape: pl.BlockSpec(shape, lambda i: (0,) * len(shape))
    by_col = lambda n: pl.BlockSpec((n, block), lambda i: (0, i))

    stamped = pl.pallas_call(
        stamp_kernel, out_shape=bf(n_tok + 8, width), compiler_params=params(16), name="stamp"
    )(meta, tokens)
    grads = pl.pallas_call(
        dequant_kernel, out_shape=bf(n_tok, width), compiler_params=params(16), name="dequant"
    )(grad_codes, grad_scales)

    held_t, held_g = {0: stamped}, {0: grads}

    def hop(held, n):
        held[n] = ring_permute(held[n - 1], 1)
        held[-n] = ring_permute(held[1 - n], -1)

    for n in (1, 2):
        hop(held_t, n)
        hop(held_g, n)
    hop(held_t, 3)

    def pick_tokens(early, backs, *rest):
        picked = [bf(N_EARLY, width)] * 2 + [bf(2 * N_REST, width)]
        return pl.pallas_call(
            functools.partial(pick_tokens_kernel, early),
            in_specs=[smem] + [vmem] * (len(backs) + len(rest)),
            out_specs=[vmem] * (4 if early else 3),
            out_shape=(picked if early else [bf(N_LATE + N_REST, width)] * 2)
            + [f32(16 * len(backs), n_tok)],
            compiler_params=params(32),
            name="pick_tokens",
        )(place, *[held_t[b] for b in backs], *rest)

    def pick_grads(early, info, backs, *rest):
        picked = [bf(N_EARLY, width)] * 2 + [bf(2 * N_REST, width)]
        return pl.pallas_call(
            functools.partial(pick_grads_kernel, early),
            out_shape=picked if early else [bf(N_LATE + N_REST, width)] * 2,
            compiler_params=params(32),
            name="pick_grads",
        )(info, *[held_g[b] for b in backs], *rest)

    def forward(own, other, name):
        half = own.shape[0]
        rows = 2 * half
        return pl.pallas_call(
            forward_kernel,
            grid=(steps,),
            in_specs=[whole(half, width), whole(half, width), by_col(width), by_col(width)],
            out_specs=[whole(rows, width), by_col(rows), by_col(rows), by_col(rows)],
            out_shape=[bf(rows, width), bf(rows, hidden), f32(rows, hidden), f32(rows, hidden)],
            compiler_params=params(32),
            name=name,
        )(own, other, gate_w, up_w)

    def pair_specs(rows):
        return [
            whole(rows, hidden),
            whole(rows, hidden),
            pl.BlockSpec((QCOLS, hidden), lambda i: (i, 0)),
            pl.BlockSpec((QCOLS, hidden), lambda i: (i, 0)),
        ]

    own_t, send_t, rest_t, info = pick_tokens(True, EARLY)
    own_t, send_t, rest_t, info = tie(held_g, EARLY, own_t, send_t, rest_t, info)
    hop(held_g, 3)
    in_e, act_e, dgate_e, dup_e = forward(own_t, swap_cores(send_t), "forward_early")
    own_g, send_g, rest_g = pick_grads(True, info, EARLY)
    own_g, send_g, rest_g = tie(held_t, (3, -3), own_g, send_g, rest_g)
    held_t[4] = ring_permute(held_t[3], 1)
    act_e, dgate_e, dup_e = tie(held_g, (3, -3), act_e, dgate_e, dup_e)
    held_g[4] = ring_permute(held_g[-3], -1)
    n_early = 2 * N_EARLY
    grad_e, gg_e, gu_e = pl.pallas_call(
        hidden_grads,
        out_shape=[bf(n_early, width), bf(n_early, hidden), bf(n_early, hidden)],
        compiler_params=params(32),
        name="hidden_early",
    )(own_g, swap_cores(send_g), down_w, dgate_e, dup_e)
    pair_e = pl.pallas_call(
        early_pair_kernel,
        grid=(QUARTERS,),
        in_specs=pair_specs(n_early),
        out_specs=pl.BlockSpec((n_early, QCOLS), lambda i: (0, i)),
        out_shape=bf(n_early, width),
        compiler_params=params(32),
        name="pair_early",
    )(gg_e, gu_e, gate_w, up_w)
    each = 3 * hidden // 2
    far_shapes = [bf(4, each // 2, 128)] * 4
    early = pl.pallas_call(
        early_pieces_kernel,
        in_specs=[smem] + [vmem] * 5,
        out_specs=[vmem] * 10,
        out_shape=far_shapes + [bf(4, each, 128)] * 6,
        compiler_params=params(40),
        name="early_pieces",
    )(place, in_e, grad_e, act_e, gg_e, gu_e)
    held_t[4], held_g[4], pair_e, *early = lax.optimization_barrier(
        (held_t[4], held_g[4], pair_e, *early)
    )
    far_e, near_e = early[:4], early[4:]

    own_t, send_t, info = pick_tokens(False, LATE, rest_t)
    own_g, send_g = pick_grads(False, info, LATE, rest_g)
    n_late = 2 * (N_LATE + N_REST)
    anywhere = pl.BlockSpec(memory_space=pl.ANY)
    *late, far_0, far_1, far_2, far_3 = pl.pallas_call(
        late_kernel,
        in_specs=[smem] + [vmem] * 4 + [anywhere] * 7,
        out_specs=[vmem] * 9,
        out_shape=[bf(n_late, width)] * 2 + [bf(n_late, hidden)] * 3 + far_shapes,
        scratch_shapes=[
            pltpu.VMEM((width, hidden), BF16),
            pltpu.VMEM((width, hidden), BF16),
            pltpu.VMEM((hidden, width), BF16),
        ]
        + [pltpu.VMEM((4, each // 2, 128), BF16)] * 4
        + [pltpu.SemaphoreType.DMA((steps, 3)), pltpu.SemaphoreType.DMA((4,))],
        compiler_params=params(56),
        name="late",
    )(place, own_t, swap_cores(send_t), own_g, swap_cores(send_g), gate_w, up_w, down_w, *far_e)
    far = (far_0, far_1, far_2, far_3)
    gg_l, gu_l = late[3], late[4]

    def late_pieces(nears, prior, name):
        return pl.pallas_call(
            functools.partial(late_pieces_kernel, nears),
            in_specs=[smem] + [vmem] * 5 + [pl.BlockSpec(memory_space=pl.ANY)] * len(prior),
            out_specs=[vmem] * len(prior),
            out_shape=[bf(4, each, 128)] * len(prior),
            scratch_shapes=[pltpu.VMEM((4, each, 128), BF16)] * len(prior)
            + [pltpu.SemaphoreType.DMA((len(prior),))],
            compiler_params=params(56),
            name=name,
        )(place, *late, *prior)

    one_a, three_a, one_b, three_b = late_pieces(
        (1, 3), [near_e[0], near_e[1], near_e[3], near_e[4]], "late_pieces"
    )
    got = [
        plane_permute(far[0], "x", 1),
        plane_permute(far[1], "x", -1),
        plane_permute(far[2], "y", 1),
        plane_permute(far[3], "y", -1),
    ]
    *got, one_a, gg_l, gu_l = lax.optimization_barrier((*got, one_a, gg_l, gu_l))

    pair_slabs = pl.pallas_call(
        late_pair_kernel,
        grid=(QUARTERS,),
        in_specs=[smem] + pair_specs(n_late) + [pl.BlockSpec((n_early, QCOLS), lambda i: (0, i))],
        out_specs=whole(16, SLAB, QCOLS),
        out_shape=bf(16, SLAB, QCOLS),
        scratch_shapes=[pltpu.VMEM((256, QCOLS), F32)],
        compiler_params=params(32),
        name="pair_late",
    )(place, gg_l, gu_l, gate_w, up_w, pair_e)
    pair_slabs, one_a, three_a, one_b, three_b = lax.optimization_barrier(
        (pair_slabs, one_a, three_a, one_b, three_b)
    )
    returned = exchange(pair_slabs)
    one_a = add_pieces(add_first_kernel, one_a, got[0])
    three_a = add_pieces(add_last_kernel, three_a, got[1])
    one_b = add_pieces(add_first_kernel, one_b, got[2])
    three_b = add_pieces(add_last_kernel, three_b, got[3])
    *late, one_a, three_a, one_b, three_b = lax.optimization_barrier(
        (*late, one_a, three_a, one_b, three_b)
    )
    own_a, own_b = late_pieces((0,), [near_e[2], near_e[5]], "late_own_pieces")

    parts_a = plane_sum(one_a, three_a, own_a, "x")
    parts_b = plane_sum(one_b, three_b, own_b, "y")
    gate_grad, up_grad, down_grad = pl.pallas_call(
        finish_kernel,
        out_shape=[
            jax.ShapeDtypeStruct((128, hidden), F32),
            jax.ShapeDtypeStruct((128, hidden), F32),
            jax.ShapeDtypeStruct((hidden, 128), F32),
        ],
        compiler_params=params(24),
        name="finish",
    )(*parts_a, *parts_b)

    input_grad = pl.pallas_call(
        combine_kernel,
        out_shape=jax.ShapeDtypeStruct((n_tok, width), BF16),
        compiler_params=params(32),
        name="combine",
    )(meta, returned)
    return input_grad, gate_grad[None], up_grad[None], down_grad[None]


def solution(mesh):
    in_specs = (
        P(("dp", "expert"), None),
        P(("dp", "expert"), None),
        P(("dp", "expert"), None),
        P(("dp", "expert")),
        P(("dp", "expert"), None),
        P(("dp", "expert"), None),
        P("expert", None, None),
        P("expert", None, None),
        P("expert", None, None),
    )
    out_specs = (
        P(("dp", "expert"), None),
        P("expert", "dp", None),
        P("expert", "dp", None),
        P("expert", None, "dp"),
    )
    return jax.shard_map(
        per_device, mesh=mesh, in_specs=in_specs, out_specs=out_specs, check_vma=False
    )
```

```python
import functools
import jax
import jax.numpy as jnp
from jax import lax
from jax.experimental import pallas as pl
from jax.experimental.pallas import tpu as pltpu
from jax.sharding import PartitionSpec as P

F32 = jnp.float32
BF16 = jnp.bfloat16
MB = 1024 * 1024

MAIN = 32
REST = 4
QUARTERS = 4
QCOLS = 512
SLAB = (MAIN + REST) * QUARTERS


def params(limit_mb):
    return pltpu.CompilerParams(vmem_limit_bytes=limit_mb * MB)


def iota(shape, dim):
    return lax.broadcasted_iota(jnp.int32, shape, dim)


def dot(a, b, dims=((1,), (0,))):
    return lax.dot_general(a, b, (dims, ((), ())), preferred_element_type=F32)


def quarter(q):
    return slice(q * QCOLS, (q + 1) * QCOLS)


def routing(meta_ref):
    n_tok = meta_ref.shape[1]
    mod = meta_ref[8:9, :]
    experts = iota((16, n_tok), 0)
    member = jnp.zeros((16, n_tok), F32)
    numer = jnp.zeros((16, n_tok), F32)
    denom = jnp.zeros((1, n_tok), F32)
    for k in range(4):
        hit = (meta_ref[k : k + 1, :] + 8 * mod) == experts
        weight = meta_ref[4 + k : 5 + k, :].astype(F32)
        member = member + jnp.where(hit, 1.0, 0.0)
        numer = numer + jnp.where(hit, weight, 0.0)
        denom = denom + weight
    earlier = jnp.where(iota((n_tok, n_tok), 0) < iota((n_tok, n_tok), 1), 1.0, 0.0)
    rank = dot(member.astype(BF16), earlier.astype(BF16))
    key = jnp.where(member > 0.5, rank, -1.0).astype(jnp.int32)
    return key, numer / denom


EARLY = (0, 1, -1, 2, -2)
LATE = (3, -3, 4)
N_EARLY = MAIN * len(EARLY)
N_LATE = MAIN * len(LATE)
N_REST = REST * 8


def source_of(place_ref, back, same_core):
    z, core = place_ref[2], place_ref[3]
    return lax.rem(z - back + 8, 8) * 2 + (core if same_core else 1 - core)


def stamp_kernel(meta_ref, tokens_ref, out_ref):
    n_tok = tokens_ref.shape[0]
    out_ref[:n_tok, :] = tokens_ref[...]
    first = iota((8, n_tok), 0) == 0
    stamps = []
    for k in range(8):
        value = meta_ref[k : k + 1, :]
        if k < 4:
            value = value + 8 * meta_ref[8:9, :]
        stamps.append(jnp.where(first, value, 0).astype(F32))
    stamps.append(jnp.zeros((8, tokens_ref.shape[1] - 8 * n_tok), F32))
    out_ref[n_tok:, :] = jnp.concatenate(stamps, axis=1).astype(BF16)


def dequant_kernel(codes_ref, scales_ref, out_ref):
    for b in range(scales_ref.shape[1]):
        cols = slice(b * 128, (b + 1) * 128)
        out_ref[:, cols] = (codes_ref[:, cols].astype(F32) * scales_ref[:, b : b + 1]).astype(BF16)


def picks(place_ref, block_ref):
    n_tok = block_ref.shape[0] - 8
    stamp = block_ref[n_tok:, :].astype(F32)[0:1, :]
    z, core = place_ref[2], place_ref[3]
    row = iota((8, n_tok), 0)
    expert = (2 * z + jnp.where(row == 0, core, 1 - core)).astype(F32)
    member = jnp.zeros((8, n_tok), F32)
    numer = jnp.zeros((8, n_tok), F32)
    denom = jnp.zeros((1, n_tok), F32)
    for k in range(4):
        hit = stamp[:, k * n_tok : (k + 1) * n_tok] == expert
        weight = stamp[:, (4 + k) * n_tok : (5 + k) * n_tok]
        member = member + jnp.where(hit, 1.0, 0.0)
        numer = numer + jnp.where(hit, weight, 0.0)
        denom = denom + weight
    earlier = jnp.where(iota((n_tok, n_tok), 0) < iota((n_tok, n_tok), 1), 1.0, 0.0)
    rank = dot(member.astype(BF16), earlier.astype(BF16))
    return jnp.where(member > 0.5, rank, -1.0), numer / denom


def pick_rows(key, share, block, want):
    pick = jnp.concatenate(
        [jnp.where(key[i : i + 1, :] == want.astype(F32), 1.0, 0.0) for i in range(2)], axis=0
    )
    rows = dot(pick.astype(BF16), block)
    if share is not None:
        r = want.shape[0]
        factor = jnp.concatenate(
            [
                jnp.sum(pick[i * r : (i + 1) * r] * share[i : i + 1, :], axis=1, keepdims=True)
                for i in range(2)
            ],
            axis=0,
        )
        rows = rows * factor
    return rows


def rest_want(at, n_tok):
    row = iota((N_REST, n_tok), 0)
    return jnp.where(row // REST == at, MAIN + row % REST, -2)


def pick_blocks(first_at, info, blocks, own_ref, other_ref, rest):
    for i, ((key, share), block) in enumerate(zip(info, blocks)):
        n_tok = key.shape[1]
        want = jnp.concatenate(
            [iota((MAIN, n_tok), 0), rest_want(first_at + i, n_tok)], axis=0
        )
        rows = pick_rows(key, share, block, want)
        step = MAIN + N_REST
        own_ref[i * MAIN : (i + 1) * MAIN, :] = rows[:MAIN].astype(BF16)
        other_ref[i * MAIN : (i + 1) * MAIN, :] = rows[step : step + MAIN].astype(BF16)
        last = jnp.concatenate([rows[MAIN:step], rows[step + MAIN :]], axis=0)
        rest = last if rest is None else rest + last
    return rest


def pick_tokens_kernel(early, place_ref, *refs):
    backs = EARLY if early else LATE
    blocks = refs[: len(backs)]
    n_tok = blocks[0].shape[0] - 8
    info_ref = refs[-1]
    info = []
    for i, block in enumerate(blocks):
        key, share = picks(place_ref, block)
        info_ref[16 * i : 16 * i + 8, :] = key
        info_ref[16 * i + 8 : 16 * i + 16, :] = share
        info.append((key, None))
    pick_finish(early, info, [b[:n_tok, :] for b in blocks], refs[len(backs) : -1])


def pick_grads_kernel(early, *refs):
    backs = EARLY if early else LATE
    info_ref, blocks = refs[0], refs[1 : 1 + len(backs)]
    info = [
        (info_ref[16 * i : 16 * i + 8, :], info_ref[16 * i + 8 : 16 * i + 16, :])
        for i in range(len(backs))
    ]
    pick_finish(early, info, [b[...] for b in blocks], refs[1 + len(backs) :])


def pick_finish(early, info, blocks, refs):
    if early:
        own_ref, other_ref, rest_ref = refs
        rest_ref[...] = pick_blocks(0, info, blocks, own_ref, other_ref, None).astype(BF16)
    else:
        rest_ref, own_ref, other_ref = refs
        rest = pick_blocks(
            len(EARLY), info, blocks, own_ref, other_ref, rest_ref[...].astype(F32)
        )
        own_ref[N_LATE:, :] = rest[:N_REST].astype(BF16)
        other_ref[N_LATE:, :] = rest[N_REST:].astype(BF16)


def forward_kernel(own_ref, other_ref, gate_ref, up_ref, rows_ref, act_ref, dgate_ref, dup_ref):
    @pl.when(pl.program_id(0) == 0)
    def _():
        half = own_ref.shape[0]
        rows_ref[:half, :] = own_ref[...]
        rows_ref[half:, :] = other_ref[...]

    rows = rows_ref[...]
    gate = dot(rows, gate_ref[...])
    upv = dot(rows, up_ref[...])
    sigm = jax.nn.sigmoid(gate)
    silu = gate * sigm
    act_ref[...] = (silu * upv).astype(BF16)
    dgate_ref[...] = upv * sigm * (1.0 + gate * (1.0 - sigm))
    dup_ref[...] = silu


def hidden_grads(own_ref, other_ref, down_ref, dgate_ref, dup_ref, rows_ref, gg_ref, gu_ref):
    half = own_ref.shape[0]
    rows_ref[:half, :] = own_ref[...]
    rows_ref[half:, :] = other_ref[...]
    rows = rows_ref[...]
    block = 256
    for h in range(down_ref.shape[0] // block):
        cols = slice(h * block, (h + 1) * block)
        grad_act = dot(rows, down_ref[cols, :], ((1,), (1,)))
        gg_ref[:, cols] = (grad_act * dgate_ref[:, cols]).astype(BF16)
        gu_ref[:, cols] = (grad_act * dup_ref[:, cols]).astype(BF16)


def late_kernel(place_ref, own, other, dgate, dup, in_rows, act, down, *refs):
    early, (grad_ref, gg_ref, gu_ref), outs = refs[:5], refs[5:8], refs[8:]
    half = own.shape[0]
    grad_ref[:half, :] = own[...]
    grad_ref[half:, :] = other[...]
    block = 256
    for h in range(down.shape[0] // block):
        cols = slice(h * block, (h + 1) * block)
        grad_act = dot(grad_ref[...], down[cols, :], ((1,), (1,)))
        gg_ref[:, cols] = (grad_act * dgate[:, cols]).astype(BF16)
        gu_ref[:, cols] = (grad_act * dup[:, cols]).astype(BF16)
    batches = (early, (in_rows, grad_ref, act, gg_ref, gu_ref))
    for way in range(2):
        plane_pieces(place_ref, batches, way, {2: outs[2 * way : 2 * way + 2]})


def start_copies(sources, targets, sems):
    copies = [
        pltpu.make_async_copy(source, target, sems.at[i])
        for i, (source, target) in enumerate(zip(sources, targets))
    ]
    for copy in copies:
        copy.start()
    return copies


def near_pieces_kernel(place_ref, *refs):
    sources, targets, refs = refs[:14], refs[14:18], refs[18:]
    held, outs, sems, out_sems = refs[:14], refs[14:18], refs[18], refs[19]
    loads = start_copies(sources, held, sems)
    batches, got = (held[:5], held[5:10]), held[10:]
    for copy in loads[:10]:
        copy.wait()
    stores = []
    for way in range(2):
        a, b = 2 * way, 2 * way + 1
        loads[10 + a].wait()
        loads[10 + b].wait()
        plane_pieces(
            place_ref, batches, way, {1: (outs[a],), 3: (outs[b],)}, {1: (0, got[a]), 3: (1, got[b])}
        )
        stores += start_copies(outs[a : b + 1], targets[a : b + 1], out_sems.at[way])
    for copy in stores:
        copy.wait()


def own_pieces_kernel(place_ref, *refs):
    batches, outs = (refs[:5], refs[5:10]), refs[10:]
    for way in range(2):
        plane_pieces(place_ref, batches, way, {0: (outs[way],)})


def early_pair_kernel(gg_ref, gu_ref, gate_ref, up_ref, out_ref):
    part = dot(gg_ref[...], gate_ref[...], ((1,), (1,))) + dot(
        gu_ref[...], up_ref[...], ((1,), (1,))
    )
    out_ref[...] = part.astype(BF16)


def late_pair_kernel(place_ref, gg_ref, gu_ref, gate_ref, up_ref, early_ref, slab_ref, rest):
    q = pl.program_id(0)
    part = dot(gg_ref[...], gate_ref[...], ((1,), (1,))) + dot(
        gu_ref[...], up_ref[...], ((1,), (1,))
    )
    part = part.astype(BF16)
    base = pl.multiple_of(q * MAIN, MAIN)
    row = iota((128, N_REST), 0)
    col = iota((128, N_REST), 1)
    spread = jnp.where(
        (row // 16 == col // REST) & (row % 16 == REST * q + col % REST), 1.0, 0.0
    ).astype(BF16)
    for core in range(2):
        for at, back in enumerate(EARLY):
            to = source_of(place_ref, back, core == 0)
            start = core * N_EARLY + at * MAIN
            slab_ref[to, pl.ds(base, MAIN), :] = early_ref[start : start + MAIN, :]
        first = core * (N_LATE + N_REST)
        for at, back in enumerate(LATE):
            to = source_of(place_ref, back, core == 0)
            start = first + at * MAIN
            slab_ref[to, pl.ds(base, MAIN), :] = part[start : start + MAIN]
        placed = dot(spread, part[first + N_LATE : first + N_LATE + N_REST])
        rows = slice(core * 128, (core + 1) * 128)

        @pl.when(q == 0)
        def _():
            rest[rows, :] = placed

        @pl.when(q > 0)
        def _():
            rest[rows, :] += placed

        @pl.when(q == QUARTERS - 1)
        def _():
            for at, back in enumerate(EARLY + LATE):
                to = source_of(place_ref, back, core == 0)
                start = core * 128 + at * 16
                slab_ref[to, QUARTERS * MAIN : SLAB, :] = rest[start : start + 16, :].astype(BF16)


def combine_kernel(meta_ref, slab_ref, out_ref):
    key, _ = routing(meta_ref)
    n_tok = key.shape[1]
    row = iota((MAIN, n_tok), 0)
    main = jnp.concatenate(
        [jnp.where(key[e : e + 1, :] == row, 1.0, 0.0) for e in range(16)], axis=0
    ).astype(BF16)
    last = iota((16, n_tok), 0)
    rest_rows = jnp.concatenate(
        [slab_ref[e, QUARTERS * MAIN : SLAB, :] for e in range(16)], axis=0
    )
    for q in range(QUARTERS):
        rows = jnp.concatenate(
            [slab_ref[e, q * MAIN : (q + 1) * MAIN, :] for e in range(16)], axis=0
        )
        want = jnp.where(last // REST == q, MAIN + last % REST, -2)
        rest = jnp.concatenate(
            [jnp.where(key[e : e + 1, :] == want, 1.0, 0.0) for e in range(16)], axis=0
        ).astype(BF16)
        total = dot(main, rows, ((0,), (0,))) + dot(rest, rest_rows, ((0,), (0,)))
        out_ref[:, quarter(q)] = total.astype(BF16)


def plane_pieces(place_ref, batches, way, outs, got=None):
    hidden = batches[0][2].shape[1]
    half = hidden // 2
    full = slice(0, hidden)
    if way == 0:
        parts = ((2, full, 1), (3, slice(0, half), 0))
    else:
        parts = ((3, slice(half, hidden), 0), (4, full, 0))
    here = (place_ref[0], place_ref[1])
    at = 0
    for small, cols, big in parts:
        smalls = [jnp.transpose(batch[small][:, cols]) for batch in batches]
        count = cols.stop - cols.start
        for near in outs:
            piece = 0.0
            for small_t, batch in zip(smalls, batches):
                blocks = []
                for o in range(4):
                    ry, rx = (o, near) if way == 0 else (near, o)
                    block = lax.rem(here[0] + ry, 4) * 4 + lax.rem(here[1] + rx, 4)
                    blocks.append(batch[big][:, pl.ds(pl.multiple_of(block * 128, 128), 128)])
                piece = piece + dot(small_t, jnp.concatenate(blocks, axis=1))
            for o in range(4):
                done = 0
                for ref in outs[near]:
                    start = max(at - done, 0)
                    stop = min(at + count - done, ref.shape[1])
                    cuts = [start, stop]
                    if got is not None:
                        side, came = got[near]
                        low, high = side * came.shape[1], (side + 1) * came.shape[1]
                        cuts = sorted({start, stop} | {c for c in (low, high) if start < c < stop})
                    for r0, r1 in zip(cuts[:-1], cuts[1:]):
                        if r0 >= r1:
                            continue
                        value = piece[r0 + done - at : r1 + done - at, o * 128 : (o + 1) * 128]
                        if got is not None and low <= r0 < high:
                            value = value + came[o, r0 - low : r1 - low, :].astype(F32)
                        ref[o, r0:r1, :] = value.astype(BF16)
                    done += ref.shape[1]
        at += count


def plane_permute(value, along, shift):
    if along == "x":
        perm = [(i, (i // 4) * 4 + (i + shift) % 4) for i in range(16)]
    else:
        perm = [(i, (i + 4 * shift) % 16) for i in range(16)]
    return lax.ppermute(value, "dp", perm)


def sum_kernel(own_ref, low_ref, high_ref, k0_ref, k1_ref, k2_ref, k3_ref):
    for i, ref in enumerate((k0_ref, k1_ref, k2_ref, k3_ref)):
        total = own_ref[i].astype(F32) + low_ref[i].astype(F32) + high_ref[i].astype(F32)
        ref[...] = total.astype(ref.dtype)


def plane_sum(one, three, own, along):
    other = "y" if along == "x" else "x"
    low = plane_permute(one, along, 1)
    high = plane_permute(three, along, -1)
    shape = own.shape[1:]
    kept = pl.pallas_call(
        sum_kernel,
        out_shape=[jax.ShapeDtypeStruct(shape, F32)] + [jax.ShapeDtypeStruct(shape, BF16)] * 3,
        compiler_params=params(24),
        name="sum_pieces",
    )(own, low, high)
    return (
        kept[0],
        plane_permute(kept[2], other, 2),
        plane_permute(kept[1], other, 1),
        plane_permute(kept[3], other, -1),
    )


def finish_kernel(*refs):
    a_refs, b_refs, (gate_ref, up_ref, down_ref) = refs[:4], refs[4:8], refs[8:]
    hidden = down_ref.shape[0]
    half = hidden // 2
    scale = 1.0 / 16

    def total(parts, rows):
        return sum(p[rows, :].astype(F32) for p in parts) * scale

    down_ref[...] = total(a_refs, slice(0, hidden))
    gate_ref[:, :half] = jnp.transpose(total(a_refs, slice(hidden, hidden + half)))
    gate_ref[:, half:] = jnp.transpose(total(b_refs, slice(0, half)))
    up_ref[...] = jnp.transpose(total(b_refs, slice(half, half + hidden)))


def exchange(value):
    return lax.all_to_all(value, "expert", split_axis=0, concat_axis=0, tiled=True)


def tie(held, backs, *others):
    tied = lax.optimization_barrier(tuple(held[b] for b in backs) + others)
    for b, value in zip(backs, tied):
        held[b] = value
    return tied[len(backs) :]


def ring_permute(value, shift):
    perm = [(i, ((i // 2 + shift) % 8) * 2 + i % 2) for i in range(16)]
    return lax.ppermute(value, "expert", perm)


def swap_cores(value):
    return lax.ppermute(value, "expert", [(i, i ^ 1) for i in range(16)])


def per_device(
    tokens, grad_codes, grad_scales, modality, expert_ids, combine, w_gate, w_up, w_down
):
    n_tok, width = tokens.shape
    hidden = w_gate.shape[2]
    dp_at = lax.axis_index("dp")
    ex_at = lax.axis_index("expert")
    place = jnp.stack([dp_at // 4, dp_at % 4, ex_at // 2, ex_at % 2]).astype(jnp.int32)
    meta = jnp.concatenate(
        [expert_ids.T, combine.T, modality[None, :], jnp.zeros((7, n_tok), jnp.int32)], axis=0
    )
    gate_w, up_w, down_w = w_gate[0], w_up[0], w_down[0]
    bf = lambda *shape: jax.ShapeDtypeStruct(shape, BF16)
    f32 = lambda *shape: jax.ShapeDtypeStruct(shape, F32)
    smem = pl.BlockSpec(memory_space=pltpu.SMEM)
    vmem = pl.BlockSpec(memory_space=pltpu.VMEM)
    block = 256
    steps = hidden // block
    whole = lambda *shape: pl.BlockSpec(shape, lambda i: (0,) * len(shape))
    by_col = lambda n: pl.BlockSpec((n, block), lambda i: (0, i))

    stamped = pl.pallas_call(
        stamp_kernel, out_shape=bf(n_tok + 8, width), compiler_params=params(16), name="stamp"
    )(meta, tokens)
    grads = pl.pallas_call(
        dequant_kernel, out_shape=bf(n_tok, width), compiler_params=params(16), name="dequant"
    )(grad_codes, grad_scales)

    held_t, held_g = {0: stamped}, {0: grads}

    def hop(held, n):
        held[n] = ring_permute(held[n - 1], 1)
        held[-n] = ring_permute(held[1 - n], -1)

    for n in (1, 2):
        hop(held_t, n)
        hop(held_g, n)
    hop(held_t, 3)

    def pick_tokens(early, backs, *rest):
        picked = [bf(N_EARLY, width)] * 2 + [bf(2 * N_REST, width)]
        return pl.pallas_call(
            functools.partial(pick_tokens_kernel, early),
            in_specs=[smem] + [vmem] * (len(backs) + len(rest)),
            out_specs=[vmem] * (4 if early else 3),
            out_shape=(picked if early else [bf(N_LATE + N_REST, width)] * 2)
            + [f32(16 * len(backs), n_tok)],
            compiler_params=params(32),
            name="pick_tokens",
        )(place, *[held_t[b] for b in backs], *rest)

    def pick_grads(early, info, backs, *rest):
        picked = [bf(N_EARLY, width)] * 2 + [bf(2 * N_REST, width)]
        return pl.pallas_call(
            functools.partial(pick_grads_kernel, early),
            out_shape=picked if early else [bf(N_LATE + N_REST, width)] * 2,
            compiler_params=params(32),
            name="pick_grads",
        )(info, *[held_g[b] for b in backs], *rest)

    def forward(own, other, name):
        half = own.shape[0]
        rows = 2 * half
        return pl.pallas_call(
            forward_kernel,
            grid=(steps,),
            in_specs=[whole(half, width), whole(half, width), by_col(width), by_col(width)],
            out_specs=[whole(rows, width), by_col(rows), by_col(rows), by_col(rows)],
            out_shape=[bf(rows, width), bf(rows, hidden), f32(rows, hidden), f32(rows, hidden)],
            compiler_params=params(32),
            name=name,
        )(own, other, gate_w, up_w)

    def pair_specs(rows):
        return [
            whole(rows, hidden),
            whole(rows, hidden),
            pl.BlockSpec((QCOLS, hidden), lambda i: (i, 0)),
            pl.BlockSpec((QCOLS, hidden), lambda i: (i, 0)),
        ]

    own_t, send_t, rest_t, info = pick_tokens(True, EARLY)
    own_t, send_t, rest_t, info = tie(held_g, EARLY, own_t, send_t, rest_t, info)
    hop(held_g, 3)
    in_e, act_e, dgate_e, dup_e = forward(own_t, swap_cores(send_t), "forward_early")
    own_g, send_g, rest_g = pick_grads(True, info, EARLY)
    own_g, send_g, rest_g = tie(held_t, (3, -3), own_g, send_g, rest_g)
    held_t[4] = ring_permute(held_t[3], 1)
    act_e, dgate_e, dup_e = tie(held_g, (3, -3), act_e, dgate_e, dup_e)
    held_g[4] = ring_permute(held_g[-3], -1)
    n_early = 2 * N_EARLY
    grad_e, gg_e, gu_e = pl.pallas_call(
        hidden_grads,
        out_shape=[bf(n_early, width), bf(n_early, hidden), bf(n_early, hidden)],
        compiler_params=params(32),
        name="hidden_early",
    )(own_g, swap_cores(send_g), down_w, dgate_e, dup_e)
    pair_e = pl.pallas_call(
        early_pair_kernel,
        grid=(QUARTERS,),
        in_specs=pair_specs(n_early),
        out_specs=pl.BlockSpec((n_early, QCOLS), lambda i: (0, i)),
        out_shape=bf(n_early, width),
        compiler_params=params(32),
        name="pair_early",
    )(gg_e, gu_e, gate_w, up_w)
    early = (in_e, grad_e, act_e, gg_e, gu_e)
    (pair_e,) = tie(held_t, (4,), pair_e)
    own_t, send_t, info = pick_tokens(False, LATE, rest_t)
    own_g, send_g = pick_grads(False, info, LATE, rest_g)
    in_l, act_l, dgate_l, dup_l = forward(own_t, swap_cores(send_t), "forward_late")
    n_late = 2 * (N_LATE + N_REST)
    each = 3 * hidden // 2
    grad_l, gg_l, gu_l, *far = pl.pallas_call(
        late_kernel,
        in_specs=[smem] + [vmem] * 12,
        out_specs=[vmem] * 7,
        out_shape=[bf(n_late, width)] + [bf(n_late, hidden)] * 2 + [bf(4, each // 2, 128)] * 4,
        compiler_params=params(32),
        name="late",
    )(place, own_g, swap_cores(send_g), dgate_l, dup_l, in_l, act_l, down_w, *early)
    late = (in_l, grad_l, act_l, gg_l, gu_l)

    got = [
        plane_permute(far[0], "x", 1),
        plane_permute(far[1], "x", -1),
        plane_permute(far[2], "y", 1),
        plane_permute(far[3], "y", -1),
    ]
    pair_slabs = pl.pallas_call(
        late_pair_kernel,
        grid=(QUARTERS,),
        in_specs=[smem] + pair_specs(n_late) + [pl.BlockSpec((n_early, QCOLS), lambda i: (0, i))],
        out_specs=whole(16, SLAB, QCOLS),
        out_shape=bf(16, SLAB, QCOLS),
        scratch_shapes=[pltpu.VMEM((256, QCOLS), F32)],
        compiler_params=params(32),
        cost_estimate=pl.CostEstimate(flops=10**6, bytes_accessed=10**4, transcendentals=0),
        name="pair_late",
    )(place, gg_l, gu_l, gate_w, up_w, pair_e)
    returned = exchange(pair_slabs)
    _, *got = lax.optimization_barrier((pair_slabs, *got))
    anywhere = pl.BlockSpec(memory_space=pl.ANY)
    big = bf(4, each, 128)
    one_a, three_a, one_b, three_b = pl.pallas_call(
        near_pieces_kernel,
        in_specs=[smem] + [anywhere] * 14,
        out_specs=[anywhere] * 4,
        out_shape=[bf(4, each, 128)] * 4,
        scratch_shapes=[
            pltpu.VMEM(v.shape, v.dtype) for v in (*early, *late, *got, *[big] * 4)
        ]
        + [pltpu.SemaphoreType.DMA((14,)), pltpu.SemaphoreType.DMA((2, 2))],
        compiler_params=params(56),
        name="near_pieces",
    )(place, *early, *late, *got)
    *late, one_a, three_a, one_b, three_b = lax.optimization_barrier(
        (*late, one_a, three_a, one_b, three_b)
    )
    own_a, own_b = pl.pallas_call(
        own_pieces_kernel,
        in_specs=[smem] + [vmem] * 10,
        out_specs=[vmem] * 2,
        out_shape=[bf(4, each, 128)] * 2,
        compiler_params=params(32),
        cost_estimate=pl.CostEstimate(flops=10**11, bytes_accessed=3 * 10**8, transcendentals=0),
        name="own_pieces",
    )(place, *early, *late)

    parts_a = plane_sum(one_a, three_a, own_a, "x")
    parts_b = plane_sum(one_b, three_b, own_b, "y")
    gate_grad, up_grad, down_grad = pl.pallas_call(
        finish_kernel,
        out_shape=[
            jax.ShapeDtypeStruct((128, hidden), F32),
            jax.ShapeDtypeStruct((128, hidden), F32),
            jax.ShapeDtypeStruct((hidden, 128), F32),
        ],
        compiler_params=params(24),
        name="finish",
    )(*parts_a, *parts_b)

    input_grad = pl.pallas_call(
        combine_kernel,
        out_shape=jax.ShapeDtypeStruct((n_tok, width), BF16),
        compiler_params=params(32),
        name="combine",
    )(meta, returned)
    return input_grad, gate_grad[None], up_grad[None], down_grad[None]


def solution(mesh):
    in_specs = (
        P(("dp", "expert"), None),
        P(("dp", "expert"), None),
        P(("dp", "expert"), None),
        P(("dp", "expert")),
        P(("dp", "expert"), None),
        P(("dp", "expert"), None),
        P("expert", None, None),
        P("expert", None, None),
        P("expert", None, None),
    )
    out_specs = (
        P(("dp", "expert"), None),
        P("expert", "dp", None),
        P("expert", "dp", None),
        P("expert", None, "dp"),
    )
    return jax.shard_map(
        per_device, mesh=mesh, in_specs=in_specs, out_specs=out_specs, check_vma=False
    )
```

```python
import functools
import jax
import jax.numpy as jnp
from jax import lax
from jax.experimental import pallas as pl
from jax.experimental.pallas import tpu as pltpu
from jax.sharding import PartitionSpec as P

F32 = jnp.float32
BF16 = jnp.bfloat16
MB = 1024 * 1024

MAIN = 32
REST = 4
QUARTERS = 4
QCOLS = 512
SLAB = (MAIN + REST) * QUARTERS


def params(limit_mb):
    return pltpu.CompilerParams(vmem_limit_bytes=limit_mb * MB)


def iota(shape, dim):
    return lax.broadcasted_iota(jnp.int32, shape, dim)


def dot(a, b, dims=((1,), (0,))):
    return lax.dot_general(a, b, (dims, ((), ())), preferred_element_type=F32)


def quarter(q):
    return slice(q * QCOLS, (q + 1) * QCOLS)


def routing(meta_ref):
    n_tok = meta_ref.shape[1]
    mod = meta_ref[8:9, :]
    experts = iota((16, n_tok), 0)
    member = jnp.zeros((16, n_tok), F32)
    numer = jnp.zeros((16, n_tok), F32)
    denom = jnp.zeros((1, n_tok), F32)
    for k in range(4):
        hit = (meta_ref[k : k + 1, :] + 8 * mod) == experts
        weight = meta_ref[4 + k : 5 + k, :].astype(F32)
        member = member + jnp.where(hit, 1.0, 0.0)
        numer = numer + jnp.where(hit, weight, 0.0)
        denom = denom + weight
    earlier = jnp.where(iota((n_tok, n_tok), 0) < iota((n_tok, n_tok), 1), 1.0, 0.0)
    rank = dot(member.astype(BF16), earlier.astype(BF16))
    key = jnp.where(member > 0.5, rank, -1.0).astype(jnp.int32)
    return key, numer / denom


EARLY = (0, 1, -1, 2, -2)
LATE = (3, -3, 4)
N_EARLY = MAIN * len(EARLY)
N_LATE = MAIN * len(LATE)
N_REST = REST * 8


def source_of(place_ref, back, same_core):
    z, core = place_ref[2], place_ref[3]
    return lax.rem(z - back + 8, 8) * 2 + (core if same_core else 1 - core)


def stamp_kernel(meta_ref, tokens_ref, out_ref):
    n_tok = tokens_ref.shape[0]
    out_ref[:n_tok, :] = tokens_ref[...]
    first = iota((8, n_tok), 0) == 0
    stamps = []
    for k in range(8):
        value = meta_ref[k : k + 1, :]
        if k < 4:
            value = value + 8 * meta_ref[8:9, :]
        stamps.append(jnp.where(first, value, 0).astype(F32))
    stamps.append(jnp.zeros((8, tokens_ref.shape[1] - 8 * n_tok), F32))
    out_ref[n_tok:, :] = jnp.concatenate(stamps, axis=1).astype(BF16)


def dequant_kernel(codes_ref, scales_ref, out_ref):
    for b in range(scales_ref.shape[1]):
        cols = slice(b * 128, (b + 1) * 128)
        out_ref[:, cols] = (codes_ref[:, cols].astype(F32) * scales_ref[:, b : b + 1]).astype(BF16)


def picks(place_ref, block_ref):
    n_tok = block_ref.shape[0] - 8
    stamp = block_ref[n_tok:, :].astype(F32)[0:1, :]
    z, core = place_ref[2], place_ref[3]
    row = iota((8, n_tok), 0)
    expert = (2 * z + jnp.where(row == 0, core, 1 - core)).astype(F32)
    member = jnp.zeros((8, n_tok), F32)
    numer = jnp.zeros((8, n_tok), F32)
    denom = jnp.zeros((1, n_tok), F32)
    for k in range(4):
        hit = stamp[:, k * n_tok : (k + 1) * n_tok] == expert
        weight = stamp[:, (4 + k) * n_tok : (5 + k) * n_tok]
        member = member + jnp.where(hit, 1.0, 0.0)
        numer = numer + jnp.where(hit, weight, 0.0)
        denom = denom + weight
    earlier = jnp.where(iota((n_tok, n_tok), 0) < iota((n_tok, n_tok), 1), 1.0, 0.0)
    rank = dot(member.astype(BF16), earlier.astype(BF16))
    return jnp.where(member > 0.5, rank, -1.0), numer / denom


def pick_rows(key, share, block, want):
    pick = jnp.concatenate(
        [jnp.where(key[i : i + 1, :] == want.astype(F32), 1.0, 0.0) for i in range(2)], axis=0
    )
    rows = dot(pick.astype(BF16), block)
    if share is not None:
        r = want.shape[0]
        factor = jnp.concatenate(
            [
                jnp.sum(pick[i * r : (i + 1) * r] * share[i : i + 1, :], axis=1, keepdims=True)
                for i in range(2)
            ],
            axis=0,
        )
        rows = rows * factor
    return rows


def rest_want(at, n_tok):
    row = iota((N_REST, n_tok), 0)
    return jnp.where(row // REST == at, MAIN + row % REST, -2)


def pick_blocks(first_at, info, blocks, own_ref, other_ref, rest):
    for i, ((key, share), block) in enumerate(zip(info, blocks)):
        n_tok = key.shape[1]
        want = jnp.concatenate(
            [iota((MAIN, n_tok), 0), rest_want(first_at + i, n_tok)], axis=0
        )
        rows = pick_rows(key, share, block, want)
        step = MAIN + N_REST
        own_ref[i * MAIN : (i + 1) * MAIN, :] = rows[:MAIN].astype(BF16)
        other_ref[i * MAIN : (i + 1) * MAIN, :] = rows[step : step + MAIN].astype(BF16)
        last = jnp.concatenate([rows[MAIN:step], rows[step + MAIN :]], axis=0)
        rest = last if rest is None else rest + last
    return rest


def pick_tokens_kernel(early, place_ref, *refs):
    backs = EARLY if early else LATE
    blocks = refs[: len(backs)]
    n_tok = blocks[0].shape[0] - 8
    info_ref = refs[-1]
    info = []
    for i, block in enumerate(blocks):
        key, share = picks(place_ref, block)
        info_ref[16 * i : 16 * i + 8, :] = key
        info_ref[16 * i + 8 : 16 * i + 16, :] = share
        info.append((key, None))
    pick_finish(early, info, [b[:n_tok, :] for b in blocks], refs[len(backs) : -1])


def pick_grads_kernel(early, *refs):
    backs = EARLY if early else LATE
    info_ref, blocks = refs[0], refs[1 : 1 + len(backs)]
    info = [
        (info_ref[16 * i : 16 * i + 8, :], info_ref[16 * i + 8 : 16 * i + 16, :])
        for i in range(len(backs))
    ]
    pick_finish(early, info, [b[...] for b in blocks], refs[1 + len(backs) :])


def pick_finish(early, info, blocks, refs):
    if early:
        own_ref, other_ref, rest_ref = refs
        rest_ref[...] = pick_blocks(0, info, blocks, own_ref, other_ref, None).astype(BF16)
    else:
        rest_ref, own_ref, other_ref = refs
        rest = pick_blocks(
            len(EARLY), info, blocks, own_ref, other_ref, rest_ref[...].astype(F32)
        )
        own_ref[N_LATE:, :] = rest[:N_REST].astype(BF16)
        other_ref[N_LATE:, :] = rest[N_REST:].astype(BF16)


def forward_kernel(own_ref, other_ref, gate_ref, up_ref, rows_ref, act_ref, dgate_ref, dup_ref):
    @pl.when(pl.program_id(0) == 0)
    def _():
        half = own_ref.shape[0]
        rows_ref[:half, :] = own_ref[...]
        rows_ref[half:, :] = other_ref[...]

    rows = rows_ref[...]
    gate = dot(rows, gate_ref[...])
    upv = dot(rows, up_ref[...])
    sigm = jax.nn.sigmoid(gate)
    silu = gate * sigm
    act_ref[...] = (silu * upv).astype(BF16)
    dgate_ref[...] = upv * sigm * (1.0 + gate * (1.0 - sigm))
    dup_ref[...] = silu


def hidden_grads(own_ref, other_ref, down_ref, dgate_ref, dup_ref, rows_ref, gg_ref, gu_ref):
    half = own_ref.shape[0]
    rows_ref[:half, :] = own_ref[...]
    rows_ref[half:, :] = other_ref[...]
    rows = rows_ref[...]
    block = 256
    for h in range(down_ref.shape[0] // block):
        cols = slice(h * block, (h + 1) * block)
        grad_act = dot(rows, down_ref[cols, :], ((1,), (1,)))
        gg_ref[:, cols] = (grad_act * dgate_ref[:, cols]).astype(BF16)
        gu_ref[:, cols] = (grad_act * dup_ref[:, cols]).astype(BF16)


def late_kernel(place_ref, own, other, dgate, dup, in_rows, act, down, *refs):
    prior, (grad_ref, gg_ref, gu_ref), outs = refs[:4], refs[4:7], refs[7:]
    half = own.shape[0]
    grad_ref[:half, :] = own[...]
    grad_ref[half:, :] = other[...]
    block = 256
    for h in range(down.shape[0] // block):
        cols = slice(h * block, (h + 1) * block)
        grad_act = dot(grad_ref[...], down[cols, :], ((1,), (1,)))
        gg_ref[:, cols] = (grad_act * dgate[:, cols]).astype(BF16)
        gu_ref[:, cols] = (grad_act * dup[:, cols]).astype(BF16)
    batches = ((in_rows, grad_ref, act, gg_ref, gu_ref),)
    for way in range(2):
        part = slice(2 * way, 2 * way + 2)
        plane_pieces(place_ref, batches, way, {2: outs[part]}, prior={2: prior[part]})


def early_pieces_kernel(place_ref, *refs):
    batches, far, near = (refs[:5],), refs[5:9], refs[9:13]
    for way in range(2):
        a, b = 2 * way, 2 * way + 1
        plane_pieces(
            place_ref, batches, way, {2: far[a : b + 1], 1: (near[a],), 3: (near[b],)}
        )


def near_pieces_kernel(place_ref, *refs):
    sources, targets, refs = refs[:13], refs[13:17], refs[17:]
    held, outs, sems, out_sems = refs[:13], refs[13:17], refs[17], refs[18]
    order = (2, 1, 5, 6, 9, 10, 3, 0, 7, 8, 11, 12, 4)
    loads = {i: pltpu.make_async_copy(sources[i], held[i], sems.at[i]) for i in order}
    for i in order:
        loads[i].start()
    batches, prior, got = (held[:5],), held[5:9], held[9:]

    def wait(*which):
        for i in which:
            if i in loads:
                loads.pop(i).wait()

    stores = []
    for way in range(2):
        a, b = 2 * way, 2 * way + 1

        def filled(near):
            i = 2 * way + near // 2
            stores.append(pltpu.make_async_copy(outs[i], targets[i], out_sems.at[i]))
            stores[-1].start()

        plane_pieces(
            place_ref,
            batches,
            way,
            {1: (outs[a],), 3: (outs[b],)},
            {1: (0, got[a]), 3: (1, got[b])},
            lambda small, big: wait(5 + a, 5 + b, 9 + a, 9 + b, small, big),
            filled,
            {1: (prior[a],), 3: (prior[b],)},
        )
    for copy in stores:
        copy.wait()


def own_pieces_kernel(place_ref, *refs):
    batches, outs = (refs[:5], refs[5:10]), refs[10:]
    for way in range(2):
        plane_pieces(place_ref, batches, way, {0: (outs[way],)})


def pair_kernel(
    place_ref, gg_e_ref, gu_e_ref, gg_l_ref, gu_l_ref, gate_ref, up_ref, slab_ref, rest
):
    q = pl.program_id(0)
    early, part = [
        (
            dot(gg[...], gate_ref[...], ((1,), (1,))) + dot(gu[...], up_ref[...], ((1,), (1,)))
        ).astype(BF16)
        for gg, gu in ((gg_e_ref, gu_e_ref), (gg_l_ref, gu_l_ref))
    ]
    base = pl.multiple_of(q * MAIN, MAIN)
    row = iota((128, N_REST), 0)
    col = iota((128, N_REST), 1)
    spread = jnp.where(
        (row // 16 == col // REST) & (row % 16 == REST * q + col % REST), 1.0, 0.0
    ).astype(BF16)
    for core in range(2):
        for at, back in enumerate(EARLY):
            to = source_of(place_ref, back, core == 0)
            start = core * N_EARLY + at * MAIN
            slab_ref[to, pl.ds(base, MAIN), :] = early[start : start + MAIN]
        first = core * (N_LATE + N_REST)
        for at, back in enumerate(LATE):
            to = source_of(place_ref, back, core == 0)
            start = first + at * MAIN
            slab_ref[to, pl.ds(base, MAIN), :] = part[start : start + MAIN]
        placed = dot(spread, part[first + N_LATE : first + N_LATE + N_REST])
        rows = slice(core * 128, (core + 1) * 128)

        @pl.when(q == 0)
        def _():
            rest[rows, :] = placed

        @pl.when(q > 0)
        def _():
            rest[rows, :] += placed

        @pl.when(q == QUARTERS - 1)
        def _():
            for at, back in enumerate(EARLY + LATE):
                to = source_of(place_ref, back, core == 0)
                start = core * 128 + at * 16
                slab_ref[to, QUARTERS * MAIN : SLAB, :] = rest[start : start + 16, :].astype(BF16)


def combine_kernel(meta_ref, slab_ref, out_ref):
    key, _ = routing(meta_ref)
    n_tok = key.shape[1]
    row = iota((MAIN, n_tok), 0)
    main = jnp.concatenate(
        [jnp.where(key[e : e + 1, :] == row, 1.0, 0.0) for e in range(16)], axis=0
    ).astype(BF16)
    last = iota((16, n_tok), 0)
    rest_rows = jnp.concatenate(
        [slab_ref[e, QUARTERS * MAIN : SLAB, :] for e in range(16)], axis=0
    )
    for q in range(QUARTERS):
        rows = jnp.concatenate(
            [slab_ref[e, q * MAIN : (q + 1) * MAIN, :] for e in range(16)], axis=0
        )
        want = jnp.where(last // REST == q, MAIN + last % REST, -2)
        rest = jnp.concatenate(
            [jnp.where(key[e : e + 1, :] == want, 1.0, 0.0) for e in range(16)], axis=0
        ).astype(BF16)
        total = dot(main, rows, ((0,), (0,))) + dot(rest, rest_rows, ((0,), (0,)))
        out_ref[:, quarter(q)] = total.astype(BF16)


def plane_pieces(place_ref, batches, way, outs, got=None, ready=None, filled=None, prior=None):
    hidden = batches[0][2].shape[1]
    half = hidden // 2
    full = slice(0, hidden)
    if way == 0:
        parts = ((2, full, 1), (3, slice(0, half), 0))
    else:
        parts = ((3, slice(half, hidden), 0), (4, full, 0))
    here = (place_ref[0], place_ref[1])
    at = 0
    for small, cols, big in parts:
        if ready is not None:
            ready(small, big)
        smalls = [jnp.transpose(batch[small][:, cols]) for batch in batches]
        count = cols.stop - cols.start
        for near in outs:
            piece = 0.0
            for small_t, batch in zip(smalls, batches):
                blocks = []
                for o in range(4):
                    ry, rx = (o, near) if way == 0 else (near, o)
                    block = lax.rem(here[0] + ry, 4) * 4 + lax.rem(here[1] + rx, 4)
                    blocks.append(batch[big][:, pl.ds(pl.multiple_of(block * 128, 128), 128)])
                piece = piece + dot(small_t, jnp.concatenate(blocks, axis=1))
            for o in range(4):
                done = 0
                for i, ref in enumerate(outs[near]):
                    start = max(at - done, 0)
                    stop = min(at + count - done, ref.shape[1])
                    cuts = [start, stop]
                    if got is not None:
                        side, came = got[near]
                        low, high = side * came.shape[1], (side + 1) * came.shape[1]
                        cuts = sorted({start, stop} | {c for c in (low, high) if start < c < stop})
                    for r0, r1 in zip(cuts[:-1], cuts[1:]):
                        if r0 >= r1:
                            continue
                        value = piece[r0 + done - at : r1 + done - at, o * 128 : (o + 1) * 128]
                        if prior is not None:
                            value = value + prior[near][i][o, r0:r1, :].astype(F32)
                        if got is not None and low <= r0 < high:
                            value = value + came[o, r0 - low : r1 - low, :].astype(F32)
                        ref[o, r0:r1, :] = value.astype(BF16)
                    done += ref.shape[1]
            if filled is not None and at > 0:
                filled(near)
        at += count


def plane_permute(value, along, shift):
    if along == "x":
        perm = [(i, (i // 4) * 4 + (i + shift) % 4) for i in range(16)]
    else:
        perm = [(i, (i + 4 * shift) % 16) for i in range(16)]
    return lax.ppermute(value, "dp", perm)


def sum_kernel(own_ref, low_ref, high_ref, k0_ref, k1_ref, k2_ref, k3_ref):
    for i, ref in enumerate((k0_ref, k1_ref, k2_ref, k3_ref)):
        total = own_ref[i].astype(F32) + low_ref[i].astype(F32) + high_ref[i].astype(F32)
        ref[...] = total.astype(ref.dtype)


def plane_sum(one, three, own, along):
    other = "y" if along == "x" else "x"
    low = plane_permute(one, along, 1)
    high = plane_permute(three, along, -1)
    shape = own.shape[1:]
    kept = pl.pallas_call(
        sum_kernel,
        out_shape=[jax.ShapeDtypeStruct(shape, F32)] + [jax.ShapeDtypeStruct(shape, BF16)] * 3,
        compiler_params=params(24),
        name="sum_pieces",
    )(own, low, high)
    return (
        kept[0],
        plane_permute(kept[2], other, 2),
        plane_permute(kept[1], other, 1),
        plane_permute(kept[3], other, -1),
    )


def finish_kernel(*refs):
    a_refs, b_refs, (gate_ref, up_ref, down_ref) = refs[:4], refs[4:8], refs[8:]
    hidden = down_ref.shape[0]
    half = hidden // 2
    scale = 1.0 / 16

    def total(parts, rows):
        return sum(p[rows, :].astype(F32) for p in parts) * scale

    down_ref[...] = total(a_refs, slice(0, hidden))
    gate_ref[:, :half] = jnp.transpose(total(a_refs, slice(hidden, hidden + half)))
    gate_ref[:, half:] = jnp.transpose(total(b_refs, slice(0, half)))
    up_ref[...] = jnp.transpose(total(b_refs, slice(half, half + hidden)))


def exchange(value):
    return lax.all_to_all(value, "expert", split_axis=0, concat_axis=0, tiled=True)


def tie(held, backs, *others):
    tied = lax.optimization_barrier(tuple(held[b] for b in backs) + others)
    for b, value in zip(backs, tied):
        held[b] = value
    return tied[len(backs) :]


def ring_permute(value, shift):
    perm = [(i, ((i // 2 + shift) % 8) * 2 + i % 2) for i in range(16)]
    return lax.ppermute(value, "expert", perm)


def swap_cores(value):
    return lax.ppermute(value, "expert", [(i, i ^ 1) for i in range(16)])


def per_device(
    tokens, grad_codes, grad_scales, modality, expert_ids, combine, w_gate, w_up, w_down
):
    n_tok, width = tokens.shape
    hidden = w_gate.shape[2]
    dp_at = lax.axis_index("dp")
    ex_at = lax.axis_index("expert")
    place = jnp.stack([dp_at // 4, dp_at % 4, ex_at // 2, ex_at % 2]).astype(jnp.int32)
    meta = jnp.concatenate(
        [expert_ids.T, combine.T, modality[None, :], jnp.zeros((7, n_tok), jnp.int32)], axis=0
    )
    gate_w, up_w, down_w = w_gate[0], w_up[0], w_down[0]
    bf = lambda *shape: jax.ShapeDtypeStruct(shape, BF16)
    f32 = lambda *shape: jax.ShapeDtypeStruct(shape, F32)
    smem = pl.BlockSpec(memory_space=pltpu.SMEM)
    vmem = pl.BlockSpec(memory_space=pltpu.VMEM)
    block = 256
    steps = hidden // block
    whole = lambda *shape: pl.BlockSpec(shape, lambda i: (0,) * len(shape))
    by_col = lambda n: pl.BlockSpec((n, block), lambda i: (0, i))

    stamped = pl.pallas_call(
        stamp_kernel, out_shape=bf(n_tok + 8, width), compiler_params=params(16), name="stamp"
    )(meta, tokens)
    grads = pl.pallas_call(
        dequant_kernel, out_shape=bf(n_tok, width), compiler_params=params(16), name="dequant"
    )(grad_codes, grad_scales)

    held_t, held_g = {0: stamped}, {0: grads}

    def hop(held, n):
        held[n] = ring_permute(held[n - 1], 1)
        held[-n] = ring_permute(held[1 - n], -1)

    for n in (1, 2):
        hop(held_t, n)
        hop(held_g, n)
    hop(held_t, 3)

    def pick_tokens(early, backs, *rest):
        picked = [bf(N_EARLY, width)] * 2 + [bf(2 * N_REST, width)]
        return pl.pallas_call(
            functools.partial(pick_tokens_kernel, early),
            in_specs=[smem] + [vmem] * (len(backs) + len(rest)),
            out_specs=[vmem] * (4 if early else 3),
            out_shape=(picked if early else [bf(N_LATE + N_REST, width)] * 2)
            + [f32(16 * len(backs), n_tok)],
            compiler_params=params(32),
            name="pick_tokens",
        )(place, *[held_t[b] for b in backs], *rest)

    def pick_grads(early, info, backs, *rest):
        picked = [bf(N_EARLY, width)] * 2 + [bf(2 * N_REST, width)]
        return pl.pallas_call(
            functools.partial(pick_grads_kernel, early),
            out_shape=picked if early else [bf(N_LATE + N_REST, width)] * 2,
            compiler_params=params(32),
            name="pick_grads",
        )(info, *[held_g[b] for b in backs], *rest)

    def forward(own, other, name):
        half = own.shape[0]
        rows = 2 * half
        return pl.pallas_call(
            forward_kernel,
            grid=(steps,),
            in_specs=[whole(half, width), whole(half, width), by_col(width), by_col(width)],
            out_specs=[whole(rows, width), by_col(rows), by_col(rows), by_col(rows)],
            out_shape=[bf(rows, width), bf(rows, hidden), f32(rows, hidden), f32(rows, hidden)],
            compiler_params=params(32),
            name=name,
        )(own, other, gate_w, up_w)

    own_t, send_t, rest_t, info = pick_tokens(True, EARLY)
    own_t, send_t, rest_t, info = tie(held_g, EARLY, own_t, send_t, rest_t, info)
    hop(held_g, 3)
    in_e, act_e, dgate_e, dup_e = forward(own_t, swap_cores(send_t), "forward_early")
    own_g, send_g, rest_g = pick_grads(True, info, EARLY)
    own_g, send_g, rest_g = tie(held_t, (3, -3), own_g, send_g, rest_g)
    held_t[4] = ring_permute(held_t[3], 1)
    act_e, dgate_e, dup_e = tie(held_g, (3, -3), act_e, dgate_e, dup_e)
    held_g[4] = ring_permute(held_g[-3], -1)
    n_early = 2 * N_EARLY
    grad_e, gg_e, gu_e = pl.pallas_call(
        hidden_grads,
        out_shape=[bf(n_early, width), bf(n_early, hidden), bf(n_early, hidden)],
        compiler_params=params(32),
        name="hidden_early",
    )(own_g, swap_cores(send_g), down_w, dgate_e, dup_e)
    early = (in_e, grad_e, act_e, gg_e, gu_e)
    each = 3 * hidden // 2
    far_shapes = [bf(4, each // 2, 128)] * 4
    near_shapes = [bf(4, each, 128)] * 4
    pieces_e = pl.pallas_call(
        early_pieces_kernel,
        in_specs=[smem] + [vmem] * 5,
        out_specs=[vmem] * 8,
        out_shape=far_shapes + near_shapes,
        compiler_params=params(32),
        name="early_pieces",
    )(place, *early)
    pieces_e = tie(held_t, (4,), *pieces_e)

    own_t, send_t, info = pick_tokens(False, LATE, rest_t)
    own_g, send_g = pick_grads(False, info, LATE, rest_g)
    in_l, act_l, dgate_l, dup_l = forward(own_t, swap_cores(send_t), "forward_late")
    n_late = 2 * (N_LATE + N_REST)
    grad_l, gg_l, gu_l, *far = pl.pallas_call(
        late_kernel,
        in_specs=[smem] + [vmem] * 11,
        out_specs=[vmem] * 7,
        out_shape=[bf(n_late, width)] + [bf(n_late, hidden)] * 2 + far_shapes,
        compiler_params=params(32),
        name="late",
    )(place, own_g, swap_cores(send_g), dgate_l, dup_l, in_l, act_l, down_w, *pieces_e[:4])
    late = (in_l, grad_l, act_l, gg_l, gu_l)

    got = [
        plane_permute(far[0], "x", 1),
        plane_permute(far[1], "x", -1),
        plane_permute(far[2], "y", 1),
        plane_permute(far[3], "y", -1),
    ]
    rows_of = lambda rows: [whole(rows, hidden)] * 2
    pair_slabs = pl.pallas_call(
        pair_kernel,
        grid=(QUARTERS,),
        in_specs=[smem]
        + rows_of(2 * N_EARLY)
        + rows_of(n_late)
        + [pl.BlockSpec((QCOLS, hidden), lambda i: (i, 0))] * 2,
        out_specs=whole(16, SLAB, QCOLS),
        out_shape=bf(16, SLAB, QCOLS),
        scratch_shapes=[pltpu.VMEM((256, QCOLS), F32)],
        compiler_params=params(32),
        cost_estimate=pl.CostEstimate(flops=10**6, bytes_accessed=10**4, transcendentals=0),
        name="pair",
    )(place, gg_e, gu_e, gg_l, gu_l, gate_w, up_w)
    returned = exchange(pair_slabs)
    _, *got = lax.optimization_barrier((pair_slabs, *got))
    anywhere = pl.BlockSpec(memory_space=pl.ANY)
    one_a, three_a, one_b, three_b = pl.pallas_call(
        near_pieces_kernel,
        in_specs=[smem] + [anywhere] * 13,
        out_specs=[anywhere] * 4,
        out_shape=near_shapes,
        scratch_shapes=[
            pltpu.VMEM(v.shape, v.dtype) for v in (*late, *near_shapes, *got, *near_shapes)
        ]
        + [pltpu.SemaphoreType.DMA((13,)), pltpu.SemaphoreType.DMA((4,))],
        compiler_params=params(56),
        name="near_pieces",
    )(place, *late, *pieces_e[4:], *got)
    *late, one_a, three_a, one_b, three_b = lax.optimization_barrier(
        (*late, one_a, three_a, one_b, three_b)
    )
    own_a, own_b = pl.pallas_call(
        own_pieces_kernel,
        in_specs=[smem] + [vmem] * 10,
        out_specs=[vmem] * 2,
        out_shape=near_shapes[:2],
        compiler_params=params(32),
        cost_estimate=pl.CostEstimate(flops=10**11, bytes_accessed=3 * 10**8, transcendentals=0),
        name="own_pieces",
    )(place, *early, *late)

    parts_a = plane_sum(one_a, three_a, own_a, "x")
    parts_b = plane_sum(one_b, three_b, own_b, "y")
    gate_grad, up_grad, down_grad = pl.pallas_call(
        finish_kernel,
        out_shape=[
            jax.ShapeDtypeStruct((128, hidden), F32),
            jax.ShapeDtypeStruct((128, hidden), F32),
            jax.ShapeDtypeStruct((hidden, 128), F32),
        ],
        compiler_params=params(24),
        name="finish",
    )(*parts_a, *parts_b)

    input_grad = pl.pallas_call(
        combine_kernel,
        out_shape=jax.ShapeDtypeStruct((n_tok, width), BF16),
        compiler_params=params(32),
        name="combine",
    )(meta, returned)
    return input_grad, gate_grad[None], up_grad[None], down_grad[None]


def solution(mesh):
    in_specs = (
        P(("dp", "expert"), None),
        P(("dp", "expert"), None),
        P(("dp", "expert"), None),
        P(("dp", "expert")),
        P(("dp", "expert"), None),
        P(("dp", "expert"), None),
        P("expert", None, None),
        P("expert", None, None),
        P("expert", None, None),
    )
    out_specs = (
        P(("dp", "expert"), None),
        P("expert", "dp", None),
        P("expert", "dp", None),
        P("expert", None, "dp"),
    )
    return jax.shard_map(
        per_device, mesh=mesh, in_specs=in_specs, out_specs=out_specs, check_vma=False
    )
```

```python
import functools
import jax
import jax.numpy as jnp
from jax import lax
from jax.experimental import pallas as pl
from jax.experimental.pallas import tpu as pltpu
from jax.sharding import PartitionSpec as P

F32 = jnp.float32
BF16 = jnp.bfloat16
MB = 1024 * 1024

MAIN = 32
REST = 4
QUARTERS = 4
QCOLS = 512
SLAB = (MAIN + REST) * QUARTERS


def params(limit_mb):
    return pltpu.CompilerParams(vmem_limit_bytes=limit_mb * MB)


def iota(shape, dim):
    return lax.broadcasted_iota(jnp.int32, shape, dim)


def dot(a, b, dims=((1,), (0,))):
    return lax.dot_general(a, b, (dims, ((), ())), preferred_element_type=F32)


def quarter(q):
    return slice(q * QCOLS, (q + 1) * QCOLS)


def routing(meta_ref):
    n_tok = meta_ref.shape[1]
    mod = meta_ref[8:9, :]
    experts = iota((16, n_tok), 0)
    member = jnp.zeros((16, n_tok), F32)
    numer = jnp.zeros((16, n_tok), F32)
    denom = jnp.zeros((1, n_tok), F32)
    for k in range(4):
        hit = (meta_ref[k : k + 1, :] + 8 * mod) == experts
        weight = meta_ref[4 + k : 5 + k, :].astype(F32)
        member = member + jnp.where(hit, 1.0, 0.0)
        numer = numer + jnp.where(hit, weight, 0.0)
        denom = denom + weight
    earlier = jnp.where(iota((n_tok, n_tok), 0) < iota((n_tok, n_tok), 1), 1.0, 0.0)
    rank = dot(member.astype(BF16), earlier.astype(BF16))
    key = jnp.where(member > 0.5, rank, -1.0).astype(jnp.int32)
    return key, numer / denom


EARLY = (0, 1, -1, 2, -2)
LATE = (3, -3, 4)
N_EARLY = MAIN * len(EARLY)
N_LATE = MAIN * len(LATE)
N_REST = REST * 8


def source_of(place_ref, back, same_core):
    z, core = place_ref[2], place_ref[3]
    return lax.rem(z - back + 8, 8) * 2 + (core if same_core else 1 - core)


def stamp_kernel(meta_ref, tokens_ref, out_ref):
    n_tok = tokens_ref.shape[0]
    out_ref[:n_tok, :] = tokens_ref[...]
    first = iota((8, n_tok), 0) == 0
    stamps = []
    for k in range(8):
        value = meta_ref[k : k + 1, :]
        if k < 4:
            value = value + 8 * meta_ref[8:9, :]
        stamps.append(jnp.where(first, value, 0).astype(F32))
    stamps.append(jnp.zeros((8, tokens_ref.shape[1] - 8 * n_tok), F32))
    out_ref[n_tok:, :] = jnp.concatenate(stamps, axis=1).astype(BF16)


def dequant_kernel(codes_ref, scales_ref, out_ref):
    for b in range(scales_ref.shape[1]):
        cols = slice(b * 128, (b + 1) * 128)
        out_ref[:, cols] = (codes_ref[:, cols].astype(F32) * scales_ref[:, b : b + 1]).astype(BF16)


def picks(place_ref, block_ref):
    n_tok = block_ref.shape[0] - 8
    stamp = block_ref[n_tok:, :].astype(F32)[0:1, :]
    z, core = place_ref[2], place_ref[3]
    row = iota((8, n_tok), 0)
    expert = (2 * z + jnp.where(row == 0, core, 1 - core)).astype(F32)
    member = jnp.zeros((8, n_tok), F32)
    numer = jnp.zeros((8, n_tok), F32)
    denom = jnp.zeros((1, n_tok), F32)
    for k in range(4):
        hit = stamp[:, k * n_tok : (k + 1) * n_tok] == expert
        weight = stamp[:, (4 + k) * n_tok : (5 + k) * n_tok]
        member = member + jnp.where(hit, 1.0, 0.0)
        numer = numer + jnp.where(hit, weight, 0.0)
        denom = denom + weight
    earlier = jnp.where(iota((n_tok, n_tok), 0) < iota((n_tok, n_tok), 1), 1.0, 0.0)
    rank = dot(member.astype(BF16), earlier.astype(BF16))
    return jnp.where(member > 0.5, rank, -1.0), numer / denom


def pick_rows(key, share, block, want):
    pick = jnp.concatenate(
        [jnp.where(key[i : i + 1, :] == want.astype(F32), 1.0, 0.0) for i in range(2)], axis=0
    )
    rows = dot(pick.astype(BF16), block)
    if share is not None:
        r = want.shape[0]
        factor = jnp.concatenate(
            [
                jnp.sum(pick[i * r : (i + 1) * r] * share[i : i + 1, :], axis=1, keepdims=True)
                for i in range(2)
            ],
            axis=0,
        )
        rows = rows * factor
    return rows


def rest_want(at, n_tok):
    row = iota((N_REST, n_tok), 0)
    return jnp.where(row // REST == at, MAIN + row % REST, -2)


def pick_blocks(first_at, info, blocks, own_ref, other_ref, rest):
    for i, ((key, share), block) in enumerate(zip(info, blocks)):
        n_tok = key.shape[1]
        want = jnp.concatenate(
            [iota((MAIN, n_tok), 0), rest_want(first_at + i, n_tok)], axis=0
        )
        rows = pick_rows(key, share, block, want)
        step = MAIN + N_REST
        own_ref[i * MAIN : (i + 1) * MAIN, :] = rows[:MAIN].astype(BF16)
        other_ref[i * MAIN : (i + 1) * MAIN, :] = rows[step : step + MAIN].astype(BF16)
        last = jnp.concatenate([rows[MAIN:step], rows[step + MAIN :]], axis=0)
        rest = last if rest is None else rest + last
    return rest


def pick_tokens_kernel(early, place_ref, *refs):
    backs = EARLY if early else LATE
    blocks = refs[: len(backs)]
    n_tok = blocks[0].shape[0] - 8
    info_ref = refs[-1]
    info = []
    for i, block in enumerate(blocks):
        key, share = picks(place_ref, block)
        info_ref[16 * i : 16 * i + 8, :] = key
        info_ref[16 * i + 8 : 16 * i + 16, :] = share
        info.append((key, None))
    pick_finish(early, info, [b[:n_tok, :] for b in blocks], refs[len(backs) : -1])


def pick_grads_kernel(early, *refs):
    backs = EARLY if early else LATE
    info_ref, blocks = refs[0], refs[1 : 1 + len(backs)]
    info = [
        (info_ref[16 * i : 16 * i + 8, :], info_ref[16 * i + 8 : 16 * i + 16, :])
        for i in range(len(backs))
    ]
    pick_finish(early, info, [b[...] for b in blocks], refs[1 + len(backs) :])


def pick_finish(early, info, blocks, refs):
    if early:
        own_ref, other_ref, rest_ref = refs
        rest_ref[...] = pick_blocks(0, info, blocks, own_ref, other_ref, None).astype(BF16)
    else:
        rest_ref, own_ref, other_ref = refs
        rest = pick_blocks(
            len(EARLY), info, blocks, own_ref, other_ref, rest_ref[...].astype(F32)
        )
        own_ref[N_LATE:, :] = rest[:N_REST].astype(BF16)
        other_ref[N_LATE:, :] = rest[N_REST:].astype(BF16)


def forward_kernel(own_ref, other_ref, gate_ref, up_ref, rows_ref, act_ref, dgate_ref, dup_ref):
    @pl.when(pl.program_id(0) == 0)
    def _():
        half = own_ref.shape[0]
        rows_ref[:half, :] = own_ref[...]
        rows_ref[half:, :] = other_ref[...]

    rows = rows_ref[...]
    gate = dot(rows, gate_ref[...])
    upv = dot(rows, up_ref[...])
    sigm = jax.nn.sigmoid(gate)
    silu = gate * sigm
    act_ref[...] = (silu * upv).astype(BF16)
    dgate_ref[...] = upv * sigm * (1.0 + gate * (1.0 - sigm))
    dup_ref[...] = silu


def hidden_grads(own_ref, other_ref, down_ref, dgate_ref, dup_ref, rows_ref, gg_ref, gu_ref):
    half = own_ref.shape[0]
    rows_ref[:half, :] = own_ref[...]
    rows_ref[half:, :] = other_ref[...]
    rows = rows_ref[...]
    block = 256
    for h in range(down_ref.shape[0] // block):
        cols = slice(h * block, (h + 1) * block)
        grad_act = dot(rows, down_ref[cols, :], ((1,), (1,)))
        gg_ref[:, cols] = (grad_act * dgate_ref[:, cols]).astype(BF16)
        gu_ref[:, cols] = (grad_act * dup_ref[:, cols]).astype(BF16)


def late_kernel(place_ref, own, other, dgate, dup, in_rows, act, down, *refs):
    prior, (grad_ref, gg_ref, gu_ref), outs = refs[:4], refs[4:7], refs[7:]
    half = own.shape[0]
    grad_ref[:half, :] = own[...]
    grad_ref[half:, :] = other[...]
    block = 256
    for h in range(down.shape[0] // block):
        cols = slice(h * block, (h + 1) * block)
        grad_act = dot(grad_ref[...], down[cols, :], ((1,), (1,)))
        gg_ref[:, cols] = (grad_act * dgate[:, cols]).astype(BF16)
        gu_ref[:, cols] = (grad_act * dup[:, cols]).astype(BF16)
    batches = ((in_rows, grad_ref, act, gg_ref, gu_ref),)
    for way in range(2):
        part = slice(2 * way, 2 * way + 2)
        plane_pieces(
            place_ref,
            batches,
            way,
            first_steps(*outs[part]),
            prior=first_steps(*prior[part]),
            rows=first_rows(outs[0].shape[1]),
        )


def first_steps(up, dn):
    four, rest = pl.ds(0, 4), pl.ds(4, 4)
    return {2: (up.at[four], dn.at[four]), 1: (up.at[rest],), 3: (dn.at[rest],)}


def first_rows(part):
    return {2: (0, 2 * part), 1: (part, 2 * part), 3: (0, part)}


def second_rows(part):
    return {1: (0, part), 3: (part, 2 * part)}


def early_pieces_kernel(place_ref, *refs):
    batches, far, near = (refs[:5],), refs[5:9], refs[9:13]
    part = near[0].shape[1]
    for way in range(2):
        a, b = 2 * way, 2 * way + 1
        plane_pieces(
            place_ref, batches, way, first_steps(far[a], far[b]), rows=first_rows(part)
        )
        plane_pieces(
            place_ref, batches, way, {1: (near[a],), 3: (near[b],)}, rows=second_rows(part)
        )


def near_pieces_kernel(place_ref, *refs):
    sources, targets, refs = refs[:13], refs[13:17], refs[17:]
    held, outs, sems, out_sems = refs[:13], refs[13:17], refs[17], refs[18]
    order = (2, 1, 5, 6, 9, 10, 3, 0, 7, 8, 11, 12, 4)
    sources = sources[:9] + tuple(came.at[pl.ds(0, 4)] for came in sources[9:])
    loads = {i: pltpu.make_async_copy(sources[i], held[i], sems.at[i]) for i in order}
    for i in order:
        loads[i].start()
    batches, prior, got = (held[:5],), held[5:9], held[9:]

    def wait(*which):
        for i in which:
            if i in loads:
                loads.pop(i).wait()

    stores = []
    for way in range(2):
        a, b = 2 * way, 2 * way + 1

        def filled(near):
            i = 2 * way + near // 2
            stores.append(pltpu.make_async_copy(outs[i], targets[i], out_sems.at[i]))
            stores[-1].start()

        plane_pieces(
            place_ref,
            batches,
            way,
            {1: (outs[a],), 3: (outs[b],)},
            {1: got[a], 3: got[b]},
            lambda small, big: wait(5 + a, 5 + b, 9 + a, 9 + b, small, big),
            filled,
            {1: (prior[a],), 3: (prior[b],)},
            second_rows(outs[0].shape[1]),
        )
    for copy in stores:
        copy.wait()


def own_pieces_kernel(place_ref, *refs):
    batches, outs = (refs[:5], refs[5:10]), refs[10:]
    for way in range(2):
        plane_pieces(place_ref, batches, way, {0: (outs[way],)})


def pair_kernel(
    place_ref, gg_e_ref, gu_e_ref, gg_l_ref, gu_l_ref, gate_ref, up_ref, slab_ref, rest
):
    q = pl.program_id(0)
    early, part = [
        (
            dot(gg[...], gate_ref[...], ((1,), (1,))) + dot(gu[...], up_ref[...], ((1,), (1,)))
        ).astype(BF16)
        for gg, gu in ((gg_e_ref, gu_e_ref), (gg_l_ref, gu_l_ref))
    ]
    base = pl.multiple_of(q * MAIN, MAIN)
    row = iota((128, N_REST), 0)
    col = iota((128, N_REST), 1)
    spread = jnp.where(
        (row // 16 == col // REST) & (row % 16 == REST * q + col % REST), 1.0, 0.0
    ).astype(BF16)
    for core in range(2):
        for at, back in enumerate(EARLY):
            to = source_of(place_ref, back, core == 0)
            start = core * N_EARLY + at * MAIN
            slab_ref[to, pl.ds(base, MAIN), :] = early[start : start + MAIN]
        first = core * (N_LATE + N_REST)
        for at, back in enumerate(LATE):
            to = source_of(place_ref, back, core == 0)
            start = first + at * MAIN
            slab_ref[to, pl.ds(base, MAIN), :] = part[start : start + MAIN]
        placed = dot(spread, part[first + N_LATE : first + N_LATE + N_REST])
        rows = slice(core * 128, (core + 1) * 128)

        @pl.when(q == 0)
        def _():
            rest[rows, :] = placed

        @pl.when(q > 0)
        def _():
            rest[rows, :] += placed

        @pl.when(q == QUARTERS - 1)
        def _():
            for at, back in enumerate(EARLY + LATE):
                to = source_of(place_ref, back, core == 0)
                start = core * 128 + at * 16
                slab_ref[to, QUARTERS * MAIN : SLAB, :] = rest[start : start + 16, :].astype(BF16)


def combine_kernel(meta_ref, slab_ref, out_ref):
    key, _ = routing(meta_ref)
    n_tok = key.shape[1]
    row = iota((MAIN, n_tok), 0)
    main = jnp.concatenate(
        [jnp.where(key[e : e + 1, :] == row, 1.0, 0.0) for e in range(16)], axis=0
    ).astype(BF16)
    last = iota((16, n_tok), 0)
    rest_rows = jnp.concatenate(
        [slab_ref[e, QUARTERS * MAIN : SLAB, :] for e in range(16)], axis=0
    )
    for q in range(QUARTERS):
        rows = jnp.concatenate(
            [slab_ref[e, q * MAIN : (q + 1) * MAIN, :] for e in range(16)], axis=0
        )
        want = jnp.where(last // REST == q, MAIN + last % REST, -2)
        rest = jnp.concatenate(
            [jnp.where(key[e : e + 1, :] == want, 1.0, 0.0) for e in range(16)], axis=0
        ).astype(BF16)
        total = dot(main, rows, ((0,), (0,))) + dot(rest, rest_rows, ((0,), (0,)))
        out_ref[:, quarter(q)] = total.astype(BF16)


def plane_pieces(place_ref, batches, way, outs, got=None, ready=None, filled=None, prior=None, rows=None):
    hidden = batches[0][2].shape[1]
    half = hidden // 2
    full = slice(0, hidden)
    if way == 0:
        parts = ((2, full, 1), (3, slice(0, half), 0))
    else:
        parts = ((3, slice(half, hidden), 0), (4, full, 0))
    here = (place_ref[0], place_ref[1])
    at = 0
    for small, cols, big in parts:
        if ready is not None:
            ready(small, big)
        smalls = [jnp.transpose(batch[small][:, cols]) for batch in batches]
        count = cols.stop - cols.start
        for near in outs:
            first, last = (0, 3 * half) if rows is None else rows[near]
            a0, a1 = max(at, first), min(at + count, last)
            if a0 < a1:
                piece = 0.0
                for small_t, batch in zip(smalls, batches):
                    blocks = []
                    for o in range(4):
                        ry, rx = (o, near) if way == 0 else (near, o)
                        block = lax.rem(here[0] + ry, 4) * 4 + lax.rem(here[1] + rx, 4)
                        blocks.append(batch[big][:, pl.ds(pl.multiple_of(block * 128, 128), 128)])
                    both = jnp.concatenate(blocks, axis=1)
                    piece = piece + dot(small_t[a0 - at : a1 - at], both)
                for o in range(4):
                    part = piece[:, o * 128 : (o + 1) * 128]
                    low = a0 - first
                    done = 0
                    for i, ref in enumerate(outs[near]):
                        start = max(low - done, 0)
                        stop = min(low + a1 - a0 - done, ref.shape[1])
                        if start < stop:
                            value = part[start + done - low : stop + done - low]
                            for more in (prior and prior[near][i], got and got[near]):
                                if more is not None:
                                    value = value + more[o, start:stop, :].astype(F32)
                            ref[o, start:stop, :] = value.astype(BF16)
                        done += ref.shape[1]
            if filled is not None and at > 0:
                filled(near)
        at += count


def plane_permute(value, along, shift):
    if along == "x":
        perm = [(i, (i // 4) * 4 + (i + shift) % 4) for i in range(16)]
    else:
        perm = [(i, (i + 4 * shift) % 16) for i in range(16)]
    return lax.ppermute(value, "dp", perm)


def sum_kernel(own_ref, low_ref, high_ref, up_ref, dn_ref, k0_ref, k1_ref, k2_ref, k3_ref):
    part = low_ref.shape[1]
    for i, ref in enumerate((k0_ref, k1_ref, k2_ref, k3_ref)):
        for rows, one, two in (
            (slice(0, part), low_ref[i], dn_ref[4 + i]),
            (slice(part, 2 * part), high_ref[i], up_ref[4 + i]),
        ):
            total = own_ref[i, rows, :].astype(F32) + one.astype(F32) + two.astype(F32)
            ref[rows, :] = total.astype(ref.dtype)


def plane_sum(one, three, own, up, dn, along):
    other = "y" if along == "x" else "x"
    low = plane_permute(one, along, 1)
    high = plane_permute(three, along, -1)
    shape = own.shape[1:]
    kept = pl.pallas_call(
        sum_kernel,
        out_shape=[jax.ShapeDtypeStruct(shape, F32)] + [jax.ShapeDtypeStruct(shape, BF16)] * 3,
        compiler_params=params(24),
        name="sum_pieces",
    )(own, low, high, up, dn)
    return (
        kept[0],
        plane_permute(kept[2], other, 2),
        plane_permute(kept[1], other, 1),
        plane_permute(kept[3], other, -1),
    )


def finish_kernel(*refs):
    a_refs, b_refs, (gate_ref, up_ref, down_ref) = refs[:4], refs[4:8], refs[8:]
    hidden = down_ref.shape[0]
    half = hidden // 2
    scale = 1.0 / 16

    def total(parts, rows):
        return sum(p[rows, :].astype(F32) for p in parts) * scale

    down_ref[...] = total(a_refs, slice(0, hidden))
    gate_ref[:, :half] = jnp.transpose(total(a_refs, slice(hidden, hidden + half)))
    gate_ref[:, half:] = jnp.transpose(total(b_refs, slice(0, half)))
    up_ref[...] = jnp.transpose(total(b_refs, slice(half, half + hidden)))


def exchange(value):
    return lax.all_to_all(value, "expert", split_axis=0, concat_axis=0, tiled=True)


def tie(held, backs, *others):
    tied = lax.optimization_barrier(tuple(held[b] for b in backs) + others)
    for b, value in zip(backs, tied):
        held[b] = value
    return tied[len(backs) :]


def ring_permute(value, shift):
    perm = [(i, ((i // 2 + shift) % 8) * 2 + i % 2) for i in range(16)]
    return lax.ppermute(value, "expert", perm)


def swap_cores(value):
    return lax.ppermute(value, "expert", [(i, i ^ 1) for i in range(16)])


def per_device(
    tokens, grad_codes, grad_scales, modality, expert_ids, combine, w_gate, w_up, w_down
):
    n_tok, width = tokens.shape
    hidden = w_gate.shape[2]
    dp_at = lax.axis_index("dp")
    ex_at = lax.axis_index("expert")
    place = jnp.stack([dp_at // 4, dp_at % 4, ex_at // 2, ex_at % 2]).astype(jnp.int32)
    meta = jnp.concatenate(
        [expert_ids.T, combine.T, modality[None, :], jnp.zeros((7, n_tok), jnp.int32)], axis=0
    )
    gate_w, up_w, down_w = w_gate[0], w_up[0], w_down[0]
    bf = lambda *shape: jax.ShapeDtypeStruct(shape, BF16)
    f32 = lambda *shape: jax.ShapeDtypeStruct(shape, F32)
    smem = pl.BlockSpec(memory_space=pltpu.SMEM)
    vmem = pl.BlockSpec(memory_space=pltpu.VMEM)
    block = 256
    steps = hidden // block
    whole = lambda *shape: pl.BlockSpec(shape, lambda i: (0,) * len(shape))
    by_col = lambda n: pl.BlockSpec((n, block), lambda i: (0, i))

    stamped = pl.pallas_call(
        stamp_kernel, out_shape=bf(n_tok + 8, width), compiler_params=params(16), name="stamp"
    )(meta, tokens)
    grads = pl.pallas_call(
        dequant_kernel, out_shape=bf(n_tok, width), compiler_params=params(16), name="dequant"
    )(grad_codes, grad_scales)

    held_t, held_g = {0: stamped}, {0: grads}

    def hop(held, n):
        held[n] = ring_permute(held[n - 1], 1)
        held[-n] = ring_permute(held[1 - n], -1)

    for n in (1, 2):
        hop(held_t, n)
        hop(held_g, n)
    hop(held_t, 3)

    def pick_tokens(early, backs, *rest):
        picked = [bf(N_EARLY, width)] * 2 + [bf(2 * N_REST, width)]
        return pl.pallas_call(
            functools.partial(pick_tokens_kernel, early),
            in_specs=[smem] + [vmem] * (len(backs) + len(rest)),
            out_specs=[vmem] * (4 if early else 3),
            out_shape=(picked if early else [bf(N_LATE + N_REST, width)] * 2)
            + [f32(16 * len(backs), n_tok)],
            compiler_params=params(32),
            name="pick_tokens",
        )(place, *[held_t[b] for b in backs], *rest)

    def pick_grads(early, info, backs, *rest):
        picked = [bf(N_EARLY, width)] * 2 + [bf(2 * N_REST, width)]
        return pl.pallas_call(
            functools.partial(pick_grads_kernel, early),
            out_shape=picked if early else [bf(N_LATE + N_REST, width)] * 2,
            compiler_params=params(32),
            name="pick_grads",
        )(info, *[held_g[b] for b in backs], *rest)

    def forward(own, other, name):
        half = own.shape[0]
        rows = 2 * half
        return pl.pallas_call(
            forward_kernel,
            grid=(steps,),
            in_specs=[whole(half, width), whole(half, width), by_col(width), by_col(width)],
            out_specs=[whole(rows, width), by_col(rows), by_col(rows), by_col(rows)],
            out_shape=[bf(rows, width), bf(rows, hidden), f32(rows, hidden), f32(rows, hidden)],
            compiler_params=params(32),
            name=name,
        )(own, other, gate_w, up_w)

    own_t, send_t, rest_t, info = pick_tokens(True, EARLY)
    own_t, send_t, rest_t, info = tie(held_g, EARLY, own_t, send_t, rest_t, info)
    hop(held_g, 3)
    in_e, act_e, dgate_e, dup_e = forward(own_t, swap_cores(send_t), "forward_early")
    own_g, send_g, rest_g = pick_grads(True, info, EARLY)
    own_g, send_g, rest_g = tie(held_t, (3, -3), own_g, send_g, rest_g)
    held_t[4] = ring_permute(held_t[3], 1)
    act_e, dgate_e, dup_e = tie(held_g, (3, -3), act_e, dgate_e, dup_e)
    held_g[4] = ring_permute(held_g[-3], -1)
    n_early = 2 * N_EARLY
    grad_e, gg_e, gu_e = pl.pallas_call(
        hidden_grads,
        out_shape=[bf(n_early, width), bf(n_early, hidden), bf(n_early, hidden)],
        compiler_params=params(32),
        name="hidden_early",
    )(own_g, swap_cores(send_g), down_w, dgate_e, dup_e)
    early = (in_e, grad_e, act_e, gg_e, gu_e)
    each = 3 * hidden // 2
    far_shapes = [bf(8, each // 2, 128)] * 4
    near_shapes = [bf(4, each // 2, 128)] * 4
    pieces_e = pl.pallas_call(
        early_pieces_kernel,
        in_specs=[smem] + [vmem] * 5,
        out_specs=[vmem] * 8,
        out_shape=far_shapes + near_shapes,
        compiler_params=params(32),
        name="early_pieces",
    )(place, *early)
    pieces_e = tie(held_t, (4,), *pieces_e)

    own_t, send_t, info = pick_tokens(False, LATE, rest_t)
    own_g, send_g = pick_grads(False, info, LATE, rest_g)
    in_l, act_l, dgate_l, dup_l = forward(own_t, swap_cores(send_t), "forward_late")
    n_late = 2 * (N_LATE + N_REST)
    grad_l, gg_l, gu_l, *far = pl.pallas_call(
        late_kernel,
        in_specs=[smem] + [vmem] * 11,
        out_specs=[vmem] * 7,
        out_shape=[bf(n_late, width)] + [bf(n_late, hidden)] * 2 + far_shapes,
        compiler_params=params(32),
        name="late",
    )(place, own_g, swap_cores(send_g), dgate_l, dup_l, in_l, act_l, down_w, *pieces_e[:4])
    late = (in_l, grad_l, act_l, gg_l, gu_l)

    got = [
        plane_permute(far[0], "x", 1),
        plane_permute(far[1], "x", -1),
        plane_permute(far[2], "y", 1),
        plane_permute(far[3], "y", -1),
    ]
    rows_of = lambda rows: [whole(rows, hidden)] * 2
    pair_slabs = pl.pallas_call(
        pair_kernel,
        grid=(QUARTERS,),
        in_specs=[smem]
        + rows_of(2 * N_EARLY)
        + rows_of(n_late)
        + [pl.BlockSpec((QCOLS, hidden), lambda i: (i, 0))] * 2,
        out_specs=whole(16, SLAB, QCOLS),
        out_shape=bf(16, SLAB, QCOLS),
        scratch_shapes=[pltpu.VMEM((256, QCOLS), F32)],
        compiler_params=params(32),
        cost_estimate=pl.CostEstimate(flops=10**6, bytes_accessed=10**4, transcendentals=0),
        name="pair",
    )(place, gg_e, gu_e, gg_l, gu_l, gate_w, up_w)
    returned = exchange(pair_slabs)
    _, *got = lax.optimization_barrier((pair_slabs, *got))
    anywhere = pl.BlockSpec(memory_space=pl.ANY)
    one_a, three_a, one_b, three_b = pl.pallas_call(
        near_pieces_kernel,
        in_specs=[smem] + [anywhere] * 13,
        out_specs=[anywhere] * 4,
        out_shape=near_shapes,
        scratch_shapes=[
            pltpu.VMEM(v.shape, v.dtype) for v in (*late, *near_shapes * 3)
        ]
        + [pltpu.SemaphoreType.DMA((13,)), pltpu.SemaphoreType.DMA((4,))],
        compiler_params=params(56),
        name="near_pieces",
    )(place, *late, *pieces_e[4:], *got)
    *late, one_a, three_a, one_b, three_b = lax.optimization_barrier(
        (*late, one_a, three_a, one_b, three_b)
    )
    own_a, own_b = pl.pallas_call(
        own_pieces_kernel,
        in_specs=[smem] + [vmem] * 10,
        out_specs=[vmem] * 2,
        out_shape=[bf(4, each, 128)] * 2,
        compiler_params=params(32),
        cost_estimate=pl.CostEstimate(flops=10**11, bytes_accessed=3 * 10**8, transcendentals=0),
        name="own_pieces",
    )(place, *early, *late)

    parts_a = plane_sum(one_a, three_a, own_a, got[0], got[1], "x")
    parts_b = plane_sum(one_b, three_b, own_b, got[2], got[3], "y")
    gate_grad, up_grad, down_grad = pl.pallas_call(
        finish_kernel,
        out_shape=[
            jax.ShapeDtypeStruct((128, hidden), F32),
            jax.ShapeDtypeStruct((128, hidden), F32),
            jax.ShapeDtypeStruct((hidden, 128), F32),
        ],
        compiler_params=params(24),
        name="finish",
    )(*parts_a, *parts_b)

    input_grad = pl.pallas_call(
        combine_kernel,
        out_shape=jax.ShapeDtypeStruct((n_tok, width), BF16),
        compiler_params=params(32),
        name="combine",
    )(meta, returned)
    return input_grad, gate_grad[None], up_grad[None], down_grad[None]


def solution(mesh):
    in_specs = (
        P(("dp", "expert"), None),
        P(("dp", "expert"), None),
        P(("dp", "expert"), None),
        P(("dp", "expert")),
        P(("dp", "expert"), None),
        P(("dp", "expert"), None),
        P("expert", None, None),
        P("expert", None, None),
        P("expert", None, None),
    )
    out_specs = (
        P(("dp", "expert"), None),
        P("expert", "dp", None),
        P("expert", "dp", None),
        P("expert", None, "dp"),
    )
    return jax.shard_map(
        per_device, mesh=mesh, in_specs=in_specs, out_specs=out_specs, check_vma=False
    )
```

```python
import functools
import jax
import jax.numpy as jnp
from jax import lax
from jax.experimental import pallas as pl
from jax.experimental.pallas import tpu as pltpu
from jax.sharding import PartitionSpec as P

F32 = jnp.float32
BF16 = jnp.bfloat16
MB = 1024 * 1024

MAIN = 32
REST = 4
QUARTERS = 4
QCOLS = 512
SLAB = (MAIN + REST) * QUARTERS


def params(limit_mb):
    return pltpu.CompilerParams(vmem_limit_bytes=limit_mb * MB)


def iota(shape, dim):
    return lax.broadcasted_iota(jnp.int32, shape, dim)


def dot(a, b, dims=((1,), (0,))):
    return lax.dot_general(a, b, (dims, ((), ())), preferred_element_type=F32)


def quarter(q):
    return slice(q * QCOLS, (q + 1) * QCOLS)


def routing(meta_ref):
    n_tok = meta_ref.shape[1]
    mod = meta_ref[8:9, :]
    experts = iota((16, n_tok), 0)
    member = jnp.zeros((16, n_tok), F32)
    numer = jnp.zeros((16, n_tok), F32)
    denom = jnp.zeros((1, n_tok), F32)
    for k in range(4):
        hit = (meta_ref[k : k + 1, :] + 8 * mod) == experts
        weight = meta_ref[4 + k : 5 + k, :].astype(F32)
        member = member + jnp.where(hit, 1.0, 0.0)
        numer = numer + jnp.where(hit, weight, 0.0)
        denom = denom + weight
    earlier = jnp.where(iota((n_tok, n_tok), 0) < iota((n_tok, n_tok), 1), 1.0, 0.0)
    rank = dot(member.astype(BF16), earlier.astype(BF16))
    key = jnp.where(member > 0.5, rank, -1.0).astype(jnp.int32)
    return key, numer / denom


EARLY = (0, 1, -1, 2, -2)
LATE = (3, -3, 4)
N_EARLY = MAIN * len(EARLY)
N_LATE = MAIN * len(LATE)
N_REST = REST * 8


def source_of(place_ref, back, same_core):
    z, core = place_ref[2], place_ref[3]
    return lax.rem(z - back + 8, 8) * 2 + (core if same_core else 1 - core)


def stamp_kernel(meta_ref, tokens_ref, out_ref):
    n_tok = tokens_ref.shape[0]
    out_ref[:n_tok, :] = tokens_ref[...]
    first = iota((8, n_tok), 0) == 0
    stamps = []
    for k in range(8):
        value = meta_ref[k : k + 1, :]
        if k < 4:
            value = value + 8 * meta_ref[8:9, :]
        stamps.append(jnp.where(first, value, 0).astype(F32))
    stamps.append(jnp.zeros((8, tokens_ref.shape[1] - 8 * n_tok), F32))
    out_ref[n_tok:, :] = jnp.concatenate(stamps, axis=1).astype(BF16)


def dequant_kernel(codes_ref, scales_ref, out_ref):
    for b in range(scales_ref.shape[1]):
        cols = slice(b * 128, (b + 1) * 128)
        out_ref[:, cols] = (codes_ref[:, cols].astype(F32) * scales_ref[:, b : b + 1]).astype(BF16)


def picks(place_ref, block_ref):
    n_tok = block_ref.shape[0] - 8
    stamp = block_ref[n_tok:, :].astype(F32)[0:1, :]
    z, core = place_ref[2], place_ref[3]
    row = iota((8, n_tok), 0)
    expert = (2 * z + jnp.where(row == 0, core, 1 - core)).astype(F32)
    member = jnp.zeros((8, n_tok), F32)
    numer = jnp.zeros((8, n_tok), F32)
    denom = jnp.zeros((1, n_tok), F32)
    for k in range(4):
        hit = stamp[:, k * n_tok : (k + 1) * n_tok] == expert
        weight = stamp[:, (4 + k) * n_tok : (5 + k) * n_tok]
        member = member + jnp.where(hit, 1.0, 0.0)
        numer = numer + jnp.where(hit, weight, 0.0)
        denom = denom + weight
    earlier = jnp.where(iota((n_tok, n_tok), 0) < iota((n_tok, n_tok), 1), 1.0, 0.0)
    rank = dot(member.astype(BF16), earlier.astype(BF16))
    return jnp.where(member > 0.5, rank, -1.0), numer / denom


def pick_rows(key, share, block, want):
    pick = jnp.concatenate(
        [jnp.where(key[i : i + 1, :] == want.astype(F32), 1.0, 0.0) for i in range(2)], axis=0
    )
    rows = dot(pick.astype(BF16), block)
    if share is not None:
        r = want.shape[0]
        factor = jnp.concatenate(
            [
                jnp.sum(pick[i * r : (i + 1) * r] * share[i : i + 1, :], axis=1, keepdims=True)
                for i in range(2)
            ],
            axis=0,
        )
        rows = rows * factor
    return rows


def rest_want(at, n_tok):
    row = iota((N_REST, n_tok), 0)
    return jnp.where(row // REST == at, MAIN + row % REST, -2)


def pick_blocks(first_at, info, blocks, own_ref, other_ref, rest):
    for i, ((key, share), block) in enumerate(zip(info, blocks)):
        n_tok = key.shape[1]
        want = jnp.concatenate(
            [iota((MAIN, n_tok), 0), rest_want(first_at + i, n_tok)], axis=0
        )
        rows = pick_rows(key, share, block, want)
        step = MAIN + N_REST
        own_ref[i * MAIN : (i + 1) * MAIN, :] = rows[:MAIN].astype(BF16)
        other_ref[i * MAIN : (i + 1) * MAIN, :] = rows[step : step + MAIN].astype(BF16)
        last = jnp.concatenate([rows[MAIN:step], rows[step + MAIN :]], axis=0)
        rest = last if rest is None else rest + last
    return rest


def pick_tokens_kernel(early, place_ref, *refs):
    backs = EARLY if early else LATE
    blocks = refs[: len(backs)]
    n_tok = blocks[0].shape[0] - 8
    info_ref = refs[-1]
    info = []
    for i, block in enumerate(blocks):
        key, share = picks(place_ref, block)
        info_ref[16 * i : 16 * i + 8, :] = key
        info_ref[16 * i + 8 : 16 * i + 16, :] = share
        info.append((key, None))
    pick_finish(early, info, [b[:n_tok, :] for b in blocks], refs[len(backs) : -1])


def pick_grads_kernel(early, *refs):
    backs = EARLY if early else LATE
    info_ref, blocks = refs[0], refs[1 : 1 + len(backs)]
    info = [
        (info_ref[16 * i : 16 * i + 8, :], info_ref[16 * i + 8 : 16 * i + 16, :])
        for i in range(len(backs))
    ]
    pick_finish(early, info, [b[...] for b in blocks], refs[1 + len(backs) :])


def pick_finish(early, info, blocks, refs):
    if early:
        own_ref, other_ref, rest_ref = refs
        rest_ref[...] = pick_blocks(0, info, blocks, own_ref, other_ref, None).astype(BF16)
    else:
        rest_ref, own_ref, other_ref = refs
        rest = pick_blocks(
            len(EARLY), info, blocks, own_ref, other_ref, rest_ref[...].astype(F32)
        )
        own_ref[N_LATE:, :] = rest[:N_REST].astype(BF16)
        other_ref[N_LATE:, :] = rest[N_REST:].astype(BF16)


def forward_kernel(own_ref, other_ref, gate_ref, up_ref, rows_ref, act_ref, dgate_ref, dup_ref):
    @pl.when(pl.program_id(0) == 0)
    def _():
        half = own_ref.shape[0]
        rows_ref[:half, :] = own_ref[...]
        rows_ref[half:, :] = other_ref[...]

    rows = rows_ref[...]
    gate = dot(rows, gate_ref[...])
    upv = dot(rows, up_ref[...])
    sigm = jax.nn.sigmoid(gate)
    silu = gate * sigm
    act_ref[...] = (silu * upv).astype(BF16)
    dgate_ref[...] = upv * sigm * (1.0 + gate * (1.0 - sigm))
    dup_ref[...] = silu


def hidden_grads(own_ref, other_ref, down_ref, dgate_ref, dup_ref, rows_ref, gg_ref, gu_ref):
    half = own_ref.shape[0]
    rows_ref[:half, :] = own_ref[...]
    rows_ref[half:, :] = other_ref[...]
    rows = rows_ref[...]
    block = 256
    for h in range(down_ref.shape[0] // block):
        cols = slice(h * block, (h + 1) * block)
        grad_act = dot(rows, down_ref[cols, :], ((1,), (1,)))
        gg_ref[:, cols] = (grad_act * dgate_ref[:, cols]).astype(BF16)
        gu_ref[:, cols] = (grad_act * dup_ref[:, cols]).astype(BF16)


def late_kernel(place_ref, own, other, dgate, dup, in_rows, act, down, *refs):
    prior, (grad_ref, gg_ref, gu_ref), outs = refs[:4], refs[4:7], refs[7:]
    half = own.shape[0]
    grad_ref[:half, :] = own[...]
    grad_ref[half:, :] = other[...]
    block = 256
    for h in range(down.shape[0] // block):
        cols = slice(h * block, (h + 1) * block)
        grad_act = dot(grad_ref[...], down[cols, :], ((1,), (1,)))
        gg_ref[:, cols] = (grad_act * dgate[:, cols]).astype(BF16)
        gu_ref[:, cols] = (grad_act * dup[:, cols]).astype(BF16)
    batches = ((in_rows, grad_ref, act, gg_ref, gu_ref),)
    for way in range(2):
        part = slice(2 * way, 2 * way + 2)
        plane_pieces(
            place_ref,
            batches,
            way,
            first_steps(*outs[part]),
            prior=first_steps(*prior[part]),
            rows=first_rows(outs[0].shape[1]),
        )


def first_steps(up, dn):
    four, rest = pl.ds(0, 4), pl.ds(4, 4)
    return {2: (up.at[four], dn.at[four]), 1: (up.at[rest],), 3: (dn.at[rest],)}


def first_rows(part):
    return {2: (0, 2 * part), 1: (part, 2 * part), 3: (0, part)}


def second_rows(part):
    return {1: (0, part), 3: (part, 2 * part)}


def early_pieces_kernel(place_ref, *refs):
    batches, far, near = (refs[:5],), refs[5:9], refs[9:13]
    part = near[0].shape[1]
    for way in range(2):
        a, b = 2 * way, 2 * way + 1
        plane_pieces(
            place_ref, batches, way, first_steps(far[a], far[b]), rows=first_rows(part)
        )
        plane_pieces(
            place_ref, batches, way, {1: (near[a],), 3: (near[b],)}, rows=second_rows(part)
        )


def near_pieces_kernel(way, place_ref, *refs):
    sources, targets, refs = refs[:9], refs[9:11], refs[11:]
    held, outs, sems, out_sems = refs[:9], refs[9:11], refs[11], refs[12]
    sources = sources[:7] + tuple(came.at[pl.ds(0, 4)] for came in sources[7:])
    order = (2, 1, 5, 6, 7, 8, 3, 0) if way == 0 else (3, 0, 5, 6, 7, 8, 4)
    loads = {i: pltpu.make_async_copy(sources[i], held[i], sems.at[i]) for i in order}
    for i in order:
        loads[i].start()

    def wait(*which):
        for i in which:
            if i in loads:
                loads.pop(i).wait()

    stores = []

    def filled(near):
        i = near // 2
        stores.append(pltpu.make_async_copy(outs[i], targets[i], out_sems.at[i]))
        stores[-1].start()

    plane_pieces(
        place_ref,
        (held[:5],),
        way,
        {1: (outs[0],), 3: (outs[1],)},
        {1: held[7], 3: held[8]},
        lambda small, big: wait(5, 6, 7, 8, small, big),
        filled,
        {1: (held[5],), 3: (held[6],)},
        second_rows(outs[0].shape[1]),
    )
    for copy in stores:
        copy.wait()


def own_pieces_kernel(place_ref, *refs):
    batches, outs = (refs[:5], refs[5:10]), refs[10:]
    for way in range(2):
        plane_pieces(place_ref, batches, way, {0: (outs[way],)})


def pair_kernel(
    place_ref, gg_e_ref, gu_e_ref, gg_l_ref, gu_l_ref, gate_ref, up_ref, slab_ref, rest
):
    q = pl.program_id(0)
    early, part = [
        (
            dot(gg[...], gate_ref[...], ((1,), (1,))) + dot(gu[...], up_ref[...], ((1,), (1,)))
        ).astype(BF16)
        for gg, gu in ((gg_e_ref, gu_e_ref), (gg_l_ref, gu_l_ref))
    ]
    base = pl.multiple_of(q * MAIN, MAIN)
    row = iota((128, N_REST), 0)
    col = iota((128, N_REST), 1)
    spread = jnp.where(
        (row // 16 == col // REST) & (row % 16 == REST * q + col % REST), 1.0, 0.0
    ).astype(BF16)
    for core in range(2):
        for at, back in enumerate(EARLY):
            to = source_of(place_ref, back, core == 0)
            start = core * N_EARLY + at * MAIN
            slab_ref[to, pl.ds(base, MAIN), :] = early[start : start + MAIN]
        first = core * (N_LATE + N_REST)
        for at, back in enumerate(LATE):
            to = source_of(place_ref, back, core == 0)
            start = first + at * MAIN
            slab_ref[to, pl.ds(base, MAIN), :] = part[start : start + MAIN]
        placed = dot(spread, part[first + N_LATE : first + N_LATE + N_REST])
        rows = slice(core * 128, (core + 1) * 128)

        @pl.when(q == 0)
        def _():
            rest[rows, :] = placed

        @pl.when(q > 0)
        def _():
            rest[rows, :] += placed

        @pl.when(q == QUARTERS - 1)
        def _():
            for at, back in enumerate(EARLY + LATE):
                to = source_of(place_ref, back, core == 0)
                start = core * 128 + at * 16
                slab_ref[to, QUARTERS * MAIN : SLAB, :] = rest[start : start + 16, :].astype(BF16)


def combine_kernel(meta_ref, slab_ref, out_ref):
    key, _ = routing(meta_ref)
    n_tok = key.shape[1]
    row = iota((MAIN, n_tok), 0)
    main = jnp.concatenate(
        [jnp.where(key[e : e + 1, :] == row, 1.0, 0.0) for e in range(16)], axis=0
    ).astype(BF16)
    last = iota((16, n_tok), 0)
    rest_rows = jnp.concatenate(
        [slab_ref[e, QUARTERS * MAIN : SLAB, :] for e in range(16)], axis=0
    )
    for q in range(QUARTERS):
        rows = jnp.concatenate(
            [slab_ref[e, q * MAIN : (q + 1) * MAIN, :] for e in range(16)], axis=0
        )
        want = jnp.where(last // REST == q, MAIN + last % REST, -2)
        rest = jnp.concatenate(
            [jnp.where(key[e : e + 1, :] == want, 1.0, 0.0) for e in range(16)], axis=0
        ).astype(BF16)
        total = dot(main, rows, ((0,), (0,))) + dot(rest, rest_rows, ((0,), (0,)))
        out_ref[:, quarter(q)] = total.astype(BF16)


def plane_pieces(place_ref, batches, way, outs, got=None, ready=None, filled=None, prior=None, rows=None):
    hidden = batches[0][2].shape[1]
    half = hidden // 2
    full = slice(0, hidden)
    if way == 0:
        parts = ((2, full, 1), (3, slice(0, half), 0))
    else:
        parts = ((3, slice(half, hidden), 0), (4, full, 0))
    here = (place_ref[0], place_ref[1])
    at = 0
    for small, cols, big in parts:
        if ready is not None:
            ready(small, big)
        smalls = [jnp.transpose(batch[small][:, cols]) for batch in batches]
        count = cols.stop - cols.start
        for near in outs:
            first, last = (0, 3 * half) if rows is None else rows[near]
            a0, a1 = max(at, first), min(at + count, last)
            if a0 < a1:
                piece = 0.0
                for small_t, batch in zip(smalls, batches):
                    blocks = []
                    for o in range(4):
                        ry, rx = (o, near) if way == 0 else (near, o)
                        block = lax.rem(here[0] + ry, 4) * 4 + lax.rem(here[1] + rx, 4)
                        blocks.append(batch[big][:, pl.ds(pl.multiple_of(block * 128, 128), 128)])
                    both = jnp.concatenate(blocks, axis=1)
                    piece = piece + dot(small_t[a0 - at : a1 - at], both)
                for o in range(4):
                    part = piece[:, o * 128 : (o + 1) * 128]
                    low = a0 - first
                    done = 0
                    for i, ref in enumerate(outs[near]):
                        start = max(low - done, 0)
                        stop = min(low + a1 - a0 - done, ref.shape[1])
                        if start < stop:
                            value = part[start + done - low : stop + done - low]
                            for more in (prior and prior[near][i], got and got[near]):
                                if more is not None:
                                    value = value + more[o, start:stop, :].astype(F32)
                            ref[o, start:stop, :] = value.astype(BF16)
                        done += ref.shape[1]
            if filled is not None and at > 0:
                filled(near)
        at += count


def plane_permute(value, along, shift):
    if along == "x":
        perm = [(i, (i // 4) * 4 + (i + shift) % 4) for i in range(16)]
    else:
        perm = [(i, (i + 4 * shift) % 16) for i in range(16)]
    return lax.ppermute(value, "dp", perm)


def sum_kernel(own_ref, low_ref, high_ref, up_ref, dn_ref, k0_ref, k1_ref, k2_ref, k3_ref):
    part = low_ref.shape[1]
    for i, ref in enumerate((k0_ref, k1_ref, k2_ref, k3_ref)):
        for rows, one, two in (
            (slice(0, part), low_ref[i], dn_ref[4 + i]),
            (slice(part, 2 * part), high_ref[i], up_ref[4 + i]),
        ):
            total = own_ref[i, rows, :].astype(F32) + one.astype(F32) + two.astype(F32)
            ref[rows, :] = total.astype(ref.dtype)


def plane_sum(one, three, own, up, dn, along):
    other = "y" if along == "x" else "x"
    low = plane_permute(one, along, 1)
    high = plane_permute(three, along, -1)
    shape = own.shape[1:]
    kept = pl.pallas_call(
        sum_kernel,
        out_shape=[jax.ShapeDtypeStruct(shape, F32)] + [jax.ShapeDtypeStruct(shape, BF16)] * 3,
        compiler_params=params(24),
        name="sum_pieces",
    )(own, low, high, up, dn)
    return (
        kept[0],
        plane_permute(kept[2], other, 2),
        plane_permute(kept[1], other, 1),
        plane_permute(kept[3], other, -1),
    )


def finish_kernel(*refs):
    a_refs, b_refs, (gate_ref, up_ref, down_ref) = refs[:4], refs[4:8], refs[8:]
    hidden = down_ref.shape[0]
    half = hidden // 2
    scale = 1.0 / 16

    def total(parts, rows):
        return sum(p[rows, :].astype(F32) for p in parts) * scale

    down_ref[...] = total(a_refs, slice(0, hidden))
    gate_ref[:, :half] = jnp.transpose(total(a_refs, slice(hidden, hidden + half)))
    gate_ref[:, half:] = jnp.transpose(total(b_refs, slice(0, half)))
    up_ref[...] = jnp.transpose(total(b_refs, slice(half, half + hidden)))


def exchange(value):
    return lax.all_to_all(value, "expert", split_axis=0, concat_axis=0, tiled=True)


def tie(held, backs, *others):
    tied = lax.optimization_barrier(tuple(held[b] for b in backs) + others)
    for b, value in zip(backs, tied):
        held[b] = value
    return tied[len(backs) :]


def ring_permute(value, shift):
    perm = [(i, ((i // 2 + shift) % 8) * 2 + i % 2) for i in range(16)]
    return lax.ppermute(value, "expert", perm)


def swap_cores(value):
    return lax.ppermute(value, "expert", [(i, i ^ 1) for i in range(16)])


def per_device(
    tokens, grad_codes, grad_scales, modality, expert_ids, combine, w_gate, w_up, w_down
):
    n_tok, width = tokens.shape
    hidden = w_gate.shape[2]
    dp_at = lax.axis_index("dp")
    ex_at = lax.axis_index("expert")
    place = jnp.stack([dp_at // 4, dp_at % 4, ex_at // 2, ex_at % 2]).astype(jnp.int32)
    meta = jnp.concatenate(
        [expert_ids.T, combine.T, modality[None, :], jnp.zeros((7, n_tok), jnp.int32)], axis=0
    )
    gate_w, up_w, down_w = w_gate[0], w_up[0], w_down[0]
    bf = lambda *shape: jax.ShapeDtypeStruct(shape, BF16)
    f32 = lambda *shape: jax.ShapeDtypeStruct(shape, F32)
    smem = pl.BlockSpec(memory_space=pltpu.SMEM)
    vmem = pl.BlockSpec(memory_space=pltpu.VMEM)
    block = 256
    steps = hidden // block
    whole = lambda *shape: pl.BlockSpec(shape, lambda i: (0,) * len(shape))
    by_col = lambda n: pl.BlockSpec((n, block), lambda i: (0, i))

    stamped = pl.pallas_call(
        stamp_kernel, out_shape=bf(n_tok + 8, width), compiler_params=params(16), name="stamp"
    )(meta, tokens)
    grads = pl.pallas_call(
        dequant_kernel, out_shape=bf(n_tok, width), compiler_params=params(16), name="dequant"
    )(grad_codes, grad_scales)

    held_t, held_g = {0: stamped}, {0: grads}

    def hop(held, n):
        held[n] = ring_permute(held[n - 1], 1)
        held[-n] = ring_permute(held[1 - n], -1)

    for n in (1, 2):
        hop(held_t, n)
        hop(held_g, n)
    hop(held_t, 3)

    def pick_tokens(early, backs, *rest):
        picked = [bf(N_EARLY, width)] * 2 + [bf(2 * N_REST, width)]
        return pl.pallas_call(
            functools.partial(pick_tokens_kernel, early),
            in_specs=[smem] + [vmem] * (len(backs) + len(rest)),
            out_specs=[vmem] * (4 if early else 3),
            out_shape=(picked if early else [bf(N_LATE + N_REST, width)] * 2)
            + [f32(16 * len(backs), n_tok)],
            compiler_params=params(32),
            name="pick_tokens",
        )(place, *[held_t[b] for b in backs], *rest)

    def pick_grads(early, info, backs, *rest):
        picked = [bf(N_EARLY, width)] * 2 + [bf(2 * N_REST, width)]
        return pl.pallas_call(
            functools.partial(pick_grads_kernel, early),
            out_shape=picked if early else [bf(N_LATE + N_REST, width)] * 2,
            compiler_params=params(32),
            name="pick_grads",
        )(info, *[held_g[b] for b in backs], *rest)

    def forward(own, other, name):
        half = own.shape[0]
        rows = 2 * half
        return pl.pallas_call(
            forward_kernel,
            grid=(steps,),
            in_specs=[whole(half, width), whole(half, width), by_col(width), by_col(width)],
            out_specs=[whole(rows, width), by_col(rows), by_col(rows), by_col(rows)],
            out_shape=[bf(rows, width), bf(rows, hidden), f32(rows, hidden), f32(rows, hidden)],
            compiler_params=params(32),
            name=name,
        )(own, other, gate_w, up_w)

    own_t, send_t, rest_t, info = pick_tokens(True, EARLY)
    own_t, send_t, rest_t, info = tie(held_g, EARLY, own_t, send_t, rest_t, info)
    hop(held_g, 3)
    in_e, act_e, dgate_e, dup_e = forward(own_t, swap_cores(send_t), "forward_early")
    own_g, send_g, rest_g = pick_grads(True, info, EARLY)
    own_g, send_g, rest_g = tie(held_t, (3, -3), own_g, send_g, rest_g)
    held_t[4] = ring_permute(held_t[3], 1)
    act_e, dgate_e, dup_e = tie(held_g, (3, -3), act_e, dgate_e, dup_e)
    held_g[4] = ring_permute(held_g[-3], -1)
    n_early = 2 * N_EARLY
    grad_e, gg_e, gu_e = pl.pallas_call(
        hidden_grads,
        out_shape=[bf(n_early, width), bf(n_early, hidden), bf(n_early, hidden)],
        compiler_params=params(32),
        name="hidden_early",
    )(own_g, swap_cores(send_g), down_w, dgate_e, dup_e)
    early = (in_e, grad_e, act_e, gg_e, gu_e)
    each = 3 * hidden // 2
    far_shapes = [bf(8, each // 2, 128)] * 4
    near_shapes = [bf(4, each // 2, 128)] * 4
    pieces_e = pl.pallas_call(
        early_pieces_kernel,
        in_specs=[smem] + [vmem] * 5,
        out_specs=[vmem] * 8,
        out_shape=far_shapes + near_shapes,
        compiler_params=params(32),
        name="early_pieces",
    )(place, *early)
    pieces_e = tie(held_t, (4,), *pieces_e)

    own_t, send_t, info = pick_tokens(False, LATE, rest_t)
    own_g, send_g = pick_grads(False, info, LATE, rest_g)
    in_l, act_l, dgate_l, dup_l = forward(own_t, swap_cores(send_t), "forward_late")
    n_late = 2 * (N_LATE + N_REST)
    grad_l, gg_l, gu_l, *far = pl.pallas_call(
        late_kernel,
        in_specs=[smem] + [vmem] * 11,
        out_specs=[vmem] * 7,
        out_shape=[bf(n_late, width)] + [bf(n_late, hidden)] * 2 + far_shapes,
        compiler_params=params(32),
        name="late",
    )(place, own_g, swap_cores(send_g), dgate_l, dup_l, in_l, act_l, down_w, *pieces_e[:4])
    late = (in_l, grad_l, act_l, gg_l, gu_l)

    got = [
        plane_permute(far[0], "x", 1),
        plane_permute(far[1], "x", -1),
        plane_permute(far[2], "y", 1),
        plane_permute(far[3], "y", -1),
    ]
    rows_of = lambda rows: [whole(rows, hidden)] * 2
    pair_slabs = pl.pallas_call(
        pair_kernel,
        grid=(QUARTERS,),
        in_specs=[smem]
        + rows_of(2 * N_EARLY)
        + rows_of(n_late)
        + [pl.BlockSpec((QCOLS, hidden), lambda i: (i, 0))] * 2,
        out_specs=whole(16, SLAB, QCOLS),
        out_shape=bf(16, SLAB, QCOLS),
        scratch_shapes=[pltpu.VMEM((256, QCOLS), F32)],
        compiler_params=params(32),
        cost_estimate=pl.CostEstimate(flops=10**6, bytes_accessed=10**4, transcendentals=0),
        name="pair",
    )(place, gg_e, gu_e, gg_l, gu_l, gate_w, up_w)
    returned = exchange(pair_slabs)
    _, *got = lax.optimization_barrier((pair_slabs, *got))
    anywhere = pl.BlockSpec(memory_space=pl.ANY)
    def near_pieces(way, prior, came):
        return pl.pallas_call(
            functools.partial(near_pieces_kernel, way),
            in_specs=[smem] + [anywhere] * 9,
            out_specs=[anywhere] * 2,
            out_shape=near_shapes[:2],
            scratch_shapes=[
                pltpu.VMEM(v.shape, v.dtype) for v in (*late, *near_shapes, *near_shapes[:2])
            ]
            + [pltpu.SemaphoreType.DMA((9,)), pltpu.SemaphoreType.DMA((2,))],
            compiler_params=params(56),
            name="near_pieces",
        )(place, *late, *prior, *came)

    one_a, three_a = near_pieces(0, pieces_e[4:6], got[:2])
    got[2], got[3], one_a, three_a = lax.optimization_barrier((got[2], got[3], one_a, three_a))
    one_b, three_b = near_pieces(1, pieces_e[6:], got[2:])
    *late, one_a, three_a, one_b, three_b = lax.optimization_barrier(
        (*late, one_a, three_a, one_b, three_b)
    )
    own_a, own_b = pl.pallas_call(
        own_pieces_kernel,
        in_specs=[smem] + [vmem] * 10,
        out_specs=[vmem] * 2,
        out_shape=[bf(4, each, 128)] * 2,
        compiler_params=params(32),
        cost_estimate=pl.CostEstimate(flops=10**11, bytes_accessed=3 * 10**8, transcendentals=0),
        name="own_pieces",
    )(place, *early, *late)

    parts_a = plane_sum(one_a, three_a, own_a, got[0], got[1], "x")
    parts_b = plane_sum(one_b, three_b, own_b, got[2], got[3], "y")
    gate_grad, up_grad, down_grad = pl.pallas_call(
        finish_kernel,
        out_shape=[
            jax.ShapeDtypeStruct((128, hidden), F32),
            jax.ShapeDtypeStruct((128, hidden), F32),
            jax.ShapeDtypeStruct((hidden, 128), F32),
        ],
        compiler_params=params(24),
        name="finish",
    )(*parts_a, *parts_b)

    input_grad = pl.pallas_call(
        combine_kernel,
        out_shape=jax.ShapeDtypeStruct((n_tok, width), BF16),
        compiler_params=params(32),
        name="combine",
    )(meta, returned)
    return input_grad, gate_grad[None], up_grad[None], down_grad[None]


def solution(mesh):
    in_specs = (
        P(("dp", "expert"), None),
        P(("dp", "expert"), None),
        P(("dp", "expert"), None),
        P(("dp", "expert")),
        P(("dp", "expert"), None),
        P(("dp", "expert"), None),
        P("expert", None, None),
        P("expert", None, None),
        P("expert", None, None),
    )
    out_specs = (
        P(("dp", "expert"), None),
        P("expert", "dp", None),
        P("expert", "dp", None),
        P("expert", None, "dp"),
    )
    return jax.shard_map(
        per_device, mesh=mesh, in_specs=in_specs, out_specs=out_specs, check_vma=False
    )
```
